128 devices in a mesh: seq: 32 (over y, z, core), head: 4 (over x).
Axes of the slice: x: 4, y: 4, z: 4, core: 2. Of those that a mesh axis runs over, the one named last changes fastest.
Arguments:
- first_qkv: bfloat16 [3, 2048, 3072], P(None, 'seq', 'head'), may hold values from -64 to 64
- video_qkv: bfloat16 [3, 65536, 3072], P(None, 'seq', 'head'), may hold values from -64 to 64
- head_kind: int32 [24], replicated, may hold values from 0 to 1, as said below
- out_weight: bfloat16 [3072, 3072], P('head', 'seq'), may hold values from -0.109375 to 0.109375
Outputs:
- first_out: bfloat16 [2048, 3072], P('seq', 'head')
- video_out: bfloat16 [65536, 3072], P('seq', 'head')
The draws below stay inside these ranges and needn't reach their ends.
Inputs may be any that keep to these rules, and one draw needn't show every extreme that they name: `head_kind`: 1 marks a spatial head, 0 a temporal head; each of the 4 aligned groups of 6 consecutive heads holds 2 spatial heads.
All inputs are finite; a program needn't handle non-finite values.
Results may differ from the reference program's by a relative error of at most 0.018.
Values may be sent and summed in bfloat16 or wider, within the bound.
A program may use at most 192 MiB of HBM per device.

```python
import jax
import jax.numpy as jnp
from jax import lax

D = 3072
HEADS = 24
HEAD_DIM = 128
SPATIAL = 8
F = 2048
VIDEO_FRAMES = 32
N_HEAD = 4


def draw_first_qkv(key, part):
    key = jax.random.fold_in(key, 1)
    return jnp.clip(jax.random.normal(key, (3, F, D), jnp.float32), -6.0, 6.0).astype(jnp.bfloat16)


def draw_video_qkv(key, part):
    key = jax.random.fold_in(key, 2)
    return jnp.clip(jax.random.normal(key, (3, VIDEO_FRAMES * F, D), jnp.float32), -6.0, 6.0).astype(jnp.bfloat16)


def draw_head_kind(key, part):
    key = jax.random.fold_in(key, 3)
    per_group = HEADS // N_HEAD
    spatial_group = SPATIAL // N_HEAD
    group_keys = jax.random.split(key, N_HEAD)
    shuffled = jax.vmap(lambda single: jax.random.permutation(single, per_group))(group_keys)
    return (shuffled < spatial_group).astype(jnp.int32).reshape(HEADS)


def levels(key, shape, cuts, least, top_value):
    def one(dim, parts):
        heights = jax.random.uniform(jax.random.fold_in(jax.random.fold_in(key, 6), dim), (parts,), jnp.float32, least / len(cuts), top_value / len(cuts))
        return jnp.repeat(jnp.exp(heights), shape[dim] // parts).reshape((-1,) + (1,) * (len(shape) - dim - 1))

    factor_of = one(*cuts[0])
    for cut in cuts[1:]:
        factor_of = factor_of * one(*cut)
    return factor_of


def bell_draw(rng, extent, deviation, reach, shards=(), kind=jnp.bfloat16):
    gain = levels(rng, extent, shards, -0.22, 0.18) if shards else 1.0
    values = jax.random.normal(rng, extent, jnp.float32) * deviation * gain
    return jnp.minimum(jnp.maximum(values, -reach), reach).astype(kind)


def setup_inputs(seed: int = 0) -> dict:
    keys = jax.random.split(jax.random.key(seed), 5)
    first_qkv = draw_first_qkv(jax.random.fold_in(keys[4], 71), 0)
    video_qkv = draw_video_qkv(jax.random.fold_in(keys[4], 71), 0)
    head_kind = draw_head_kind(jax.random.fold_in(keys[4], 71), 0)
    out_weight = bell_draw(keys[3], (D, D), D ** -0.5, 0.109375, ((0, 4), (1, 32)))
    return {"first_qkv": first_qkv, "video_qkv": video_qkv, "head_kind": head_kind, "out_weight": out_weight}


def normalize(scores):
    highest = jnp.max(scores, axis=-1, keepdims=True)
    raised = jnp.exp(scores - highest)
    return (raised / jnp.sum(raised, axis=-1, keepdims=True)).astype(jnp.bfloat16)


def spatial_frame(frame_block):
    queries = frame_block[0].astype(jnp.float32)
    key_rows = frame_block[1].astype(jnp.float32)
    value_rows = frame_block[2].astype(jnp.float32)
    scores = jnp.einsum("qhd,khd->hqk", queries, key_rows) * (HEAD_DIM ** -0.5)
    weights = normalize(scores)
    return jnp.einsum("hqk,khd->qhd", weights.astype(jnp.float32), value_rows).astype(jnp.bfloat16)


def temporal_head(head_block):
    queries = head_block[0].astype(jnp.float32)
    key_rows = head_block[1].astype(jnp.float32)
    value_rows = head_block[2].astype(jnp.float32)
    scores = jnp.einsum("fpd,gpd->pfg", queries, key_rows) * (HEAD_DIM ** -0.5)
    weights = normalize(scores)
    return jnp.einsum("pfg,gpd->fpd", weights.astype(jnp.float32), value_rows).astype(jnp.bfloat16)


def reference(first_qkv, video_qkv, head_kind, out_weight):
    frame_total = VIDEO_FRAMES + 1
    stacked = jnp.concatenate([first_qkv, video_qkv], axis=1).reshape(3, frame_total, F, HEADS, HEAD_DIM)
    head_order = jnp.argsort(1 - head_kind, stable=True).astype(jnp.int32)
    spatial_heads = head_order[:SPATIAL]
    temporal_heads = head_order[SPATIAL:]
    spatial_part = jnp.moveaxis(jnp.take(stacked, spatial_heads, axis=3), 1, 0)
    spatial_done = lax.map(spatial_frame, spatial_part)
    temporal_part = jnp.moveaxis(jnp.take(stacked, temporal_heads, axis=3), 4 - 1, 0)
    temporal_done = jnp.moveaxis(lax.map(temporal_head, temporal_part), 0, 2)
    attended = jnp.zeros((frame_total, F, HEADS, HEAD_DIM), jnp.bfloat16)
    attended = attended.at[:, :, spatial_heads].set(spatial_done)
    attended = attended.at[:, :, temporal_heads].set(temporal_done)
    attended = attended.reshape(frame_total * F, D)
    group_width = D // N_HEAD
    projected = jnp.zeros((frame_total * F, D), jnp.float32)
    for holder in range(N_HEAD):
        columns = attended[:, holder * group_width:(holder + 1) * group_width]
        rows_here = out_weight[holder * group_width:(holder + 1) * group_width]
        partial_value = jnp.dot(columns, rows_here, preferred_element_type=jnp.float32).astype(jnp.bfloat16)
        partial_value = lax.optimization_barrier(partial_value)
        projected = projected + partial_value.astype(jnp.float32)
    result = projected.astype(jnp.bfloat16)
    return result[:F], result[F:]
```

```python
import functools

import jax
import jax.numpy as jnp
from jax import lax
from jax.experimental import pallas as pl
from jax.experimental.pallas import tpu as pltpu
from jax.sharding import PartitionSpec as P

HEAD_DIM = 128
F = 2048
SEQ = 32
LOCAL = 6
NS = 2
NT = 4
CHUNKS = 4
TILE = 16
WIDTH = LOCAL * HEAD_DIM
SW = NS * HEAD_DIM
TW = NT * HEAD_DIM
FRAMES = SEQ + 1
ROWS = FRAMES * TILE
EXP_SCALE = HEAD_DIM ** (-0.5) * 1.4426950408889634
MASKED = -1e30
MESH = pl.DeviceIdType.MESH
NT_DIMS = (((1,), (1,)), ((), ()))


def kernel(
    kinds, first_hbm, video_hbm, kv_hbm, w_hbm, first_out, video_out,
    first, stage, spatial, kv, weight, send, recv, back, act, part_send, part_recv, out_buf, bias,
    load_sem, const_sem, send_sem, recv_sem, back_send_sem, back_recv_sem,
    sp_send_sem, sp_recv_sem, ag_send_sem, ag_recv_sem, rs_send_sem, rs_recv_sem, out_sem,
):
    s = lax.axis_index("seq")
    g = lax.axis_index("head")
    near = jnp.bitwise_xor(g, 1)
    far = 3 - g

    def load(c):
        return pltpu.make_async_copy(
            video_hbm.at[:, :, pl.ds(c * TILE, TILE)], stage.at[c % 2], load_sem.at[c % 2]
        )

    load(0).start()
    load(1).start()
    first_copy = pltpu.make_async_copy(first_hbm, first, const_sem.at[0])
    first_copy.start()
    kv_copy = pltpu.make_async_copy(kv_hbm, kv, const_sem.at[1])
    kv_copy.start()
    w_copy = pltpu.make_async_copy(w_hbm, weight, const_sem.at[2])
    w_copy.start()

    barrier = pltpu.get_barrier_semaphore()

    def greet(k, carry):
        pl.semaphore_signal(
            barrier, inc=1, device_id=(jnp.bitwise_xor(s, k), g), device_id_type=MESH
        )
        return carry

    lax.fori_loop(1, SEQ, greet, 0)
    for other in (near, far):
        pl.semaphore_signal(barrier, inc=1, device_id=(s, other), device_id_type=MESH)

    kind = [kinds[g * LOCAL + h] for h in range(LOCAL)]
    takes = []
    for slot in range(LOCAL):
        want, rank = (1, slot) if slot < NS else (0, slot - NS)
        seen = jnp.int32(0)
        row = []
        for h in range(LOCAL):
            is_kind = kind[h] == want
            row.append(jnp.logical_and(is_kind, seen == rank))
            seen = seen + jnp.where(is_kind, 1, 0)
        takes.append(row)

    def pick(slot, heads):
        low, count = (slot, 5) if slot < NS else (slot - NS, 3)
        value = heads[low]
        for h in range(low + 1, low + count):
            value = lax.select(takes[slot][h], heads[h], value)
        return value

    def split(tile):
        return [tile[:, h * HEAD_DIM : (h + 1) * HEAD_DIM] for h in range(LOCAL)]

    row_id = lax.broadcasted_iota(jnp.int32, (TILE, ROWS), 0)
    col_id = lax.broadcasted_iota(jnp.int32, (TILE, ROWS), 1)
    bias[...] = jnp.where(row_id == jnp.bitwise_and(col_id, TILE - 1), 0.0, MASKED)

    first_copy.wait()
    for c in range(CHUNKS):
        for plane in range(3):
            heads = split(first[plane, c * TILE : (c + 1) * TILE, :])
            for slot in range(NT):
                recv[c, 0, plane, :, slot * HEAD_DIM : (slot + 1) * HEAD_DIM] = pick(
                    NS + slot, heads
                )
            if plane == 0:
                for slot in range(NS):
                    act[c, 0, :, slot * HEAD_DIM : (slot + 1) * HEAD_DIM] = pick(slot, heads)

    pl.semaphore_wait(barrier, SEQ + 1)

    for c in range(CHUNKS):
        load(c).wait()

        def pack(d, carry):
            for plane in range(3):
                heads = split(stage[c % 2, plane, d])
                for slot in range(NT):
                    send[c, d, plane, :, slot * HEAD_DIM : (slot + 1) * HEAD_DIM] = pick(
                        NS + slot, heads
                    )
                start = pl.multiple_of(d * (CHUNKS * TILE) + c * TILE, TILE)
                for slot in range(NS):
                    spatial[plane, slot, pl.ds(start, TILE), :] = pick(slot, heads)
            return carry

        lax.fori_loop(0, SEQ, pack, 0)
        if c + 2 < CHUNKS:
            load(c + 2).start()

        def post(k, carry):
            d = jnp.bitwise_xor(s, k)
            pltpu.make_async_remote_copy(
                src_ref=send.at[c, d], dst_ref=recv.at[c, 1 + s],
                send_sem=send_sem.at[c], recv_sem=recv_sem.at[c],
                device_id=(d, g), device_id_type=MESH,
            ).start()
            return carry

        lax.fori_loop(1, SEQ, post, 0)
        pltpu.make_async_copy(send.at[c, s], recv.at[c, 1 + s], recv_sem.at[c]).start()

    def attend(q, k, v, mask):
        scores = lax.dot_general(q, k, NT_DIMS, preferred_element_type=jnp.float32)
        if mask is not None:
            scores = (scores.reshape(FRAMES, TILE, ROWS) + mask[None]).reshape(ROWS, ROWS)
        top = jnp.max(scores, axis=-1, keepdims=True)
        raised = jnp.exp2((scores - top) * EXP_SCALE)
        total = jnp.sum(raised, axis=-1, keepdims=True)
        mixed = jnp.dot(raised.astype(jnp.bfloat16), v, preferred_element_type=jnp.float32)
        return (mixed / total).astype(jnp.bfloat16)

    block = 256
    for h in range(NS):
        columns = slice(h * HEAD_DIM, (h + 1) * HEAD_DIM)

        def frame_block(b, carry):
            start = pl.multiple_of(b * block, block)
            mixed = attend(spatial[0, h, pl.ds(start, block), :], spatial[1, h], spatial[2, h], None)
            for dd in range(block // (CHUNKS * TILE)):
                for c in range(CHUNKS):
                    at = (dd * CHUNKS + c) * TILE
                    act[c, 1 + b * (block // (CHUNKS * TILE)) + dd, :, columns] = mixed[at : at + TILE]
            return carry

        lax.fori_loop(0, F // block, frame_block, 0)

    kv_copy.wait()
    for h in range(NS):
        columns = slice(h * HEAD_DIM, (h + 1) * HEAD_DIM)
        queries = act[:, 0, :, columns].reshape(CHUNKS * TILE, HEAD_DIM)
        mixed = attend(queries, kv[0, :, columns], kv[1, :, columns], None)
        for c in range(CHUNKS):
            act[c, 0, :, columns] = mixed[c * TILE : (c + 1) * TILE]

    sp_copy = pltpu.make_async_remote_copy(
        src_ref=act.at[:, :, :, pl.ds(0, SW)], dst_ref=act.at[:, :, :, pl.ds(WIDTH, SW)],
        send_sem=sp_send_sem, recv_sem=sp_recv_sem,
        device_id=(s, near), device_id_type=MESH,
    )
    sp_copy.start()

    def temporal(c):
        pltpu.make_async_copy(
            recv.at[c, pl.ds(1, SEQ)], recv.at[c, pl.ds(1, SEQ)], recv_sem.at[c]
        ).wait()

        def one_head(t, carry):
            columns = pl.ds(pl.multiple_of(t * HEAD_DIM, HEAD_DIM), HEAD_DIM)
            q, k, v = (
                recv[c, :, plane, :, columns].reshape(ROWS, HEAD_DIM) for plane in range(3)
            )
            mixed = attend(q, k, v, bias[...])
            back[c, :, :, columns] = mixed.reshape(FRAMES, TILE, HEAD_DIM)
            return carry

        lax.fori_loop(0, NT, one_head, 0)

        def post(k, carry):
            d = jnp.bitwise_xor(s, k)
            pltpu.make_async_remote_copy(
                src_ref=back.at[c, 1 + d], dst_ref=act.at[c, 1 + s, :, pl.ds(SW, TW)],
                send_sem=back_send_sem.at[c], recv_sem=back_recv_sem.at[c],
                device_id=(d, g), device_id_type=MESH,
            ).start()
            return carry

        lax.fori_loop(1, SEQ, post, 0)
        pltpu.make_async_copy(
            back.at[c, 1 + s], act.at[c, 1 + s, :, pl.ds(SW, TW)], back_recv_sem.at[c]
        ).start()
        act[c, 0, :, SW:WIDTH] = back[c, 0]

    def ag_copy(c):
        return pltpu.make_async_remote_copy(
            src_ref=act.at[c, :, :, pl.ds(SW, TW)], dst_ref=act.at[c, :, :, pl.ds(WIDTH + SW, TW)],
            send_sem=ag_send_sem.at[c], recv_sem=ag_recv_sem.at[c],
            device_id=(s, near), device_id_type=MESH,
        )

    def share(c):
        landed = act.at[c, pl.ds(1, SEQ), :, pl.ds(SW, TW)]
        pltpu.make_async_copy(landed, landed, back_recv_sem.at[c]).wait()
        ag_copy(c).start()

    def rs_copy(c):
        return pltpu.make_async_remote_copy(
            src_ref=part_send.at[c], dst_ref=part_recv.at[c],
            send_sem=rs_send_sem.at[c], recv_sem=rs_recv_sem.at[c],
            device_id=(s, far), device_id_type=MESH,
        )

    def project(c, which):
        return lax.dot_general(
            act[c].reshape(ROWS, 2 * WIDTH), weight[which], NT_DIMS,
            preferred_element_type=jnp.float32,
        )

    def partial(c):
        if c == 0:
            sp_copy.wait_recv()
            w_copy.wait()
        ag_copy(c).wait_recv()
        part_send[c] = project(c, 1).astype(jnp.bfloat16).reshape(FRAMES, TILE, WIDTH)
        rs_copy(c).start()

    def out_copies(c):
        return (
            pltpu.make_async_copy(
                out_buf.at[c % 2, pl.ds(1, SEQ)], video_out.at[:, pl.ds(c * TILE, TILE)],
                out_sem.at[c % 2, 0],
            ),
            pltpu.make_async_copy(
                out_buf.at[c % 2, 0], first_out.at[pl.ds(c * TILE, TILE)], out_sem.at[c % 2, 1]
            ),
        )

    def finish(c):
        rs_copy(c).wait_recv()
        if c >= 2:
            for copy in out_copies(c - 2):
                copy.wait()
        total = project(c, 0) + part_recv[c].reshape(ROWS, WIDTH).astype(jnp.float32)
        out_buf[c % 2] = total.astype(jnp.bfloat16).reshape(FRAMES, TILE, WIDTH)
        for copy in out_copies(c):
            copy.start()

    for step in range(CHUNKS + 3):
        if step < CHUNKS:
            temporal(step)
        if 0 <= step - 1 < CHUNKS:
            share(step - 1)
        if 0 <= step - 2 < CHUNKS:
            partial(step - 2)
        if 0 <= step - 3 < CHUNKS:
            finish(step - 3)

    for c in range(CHUNKS):
        sent = send.at[c, pl.ds(0, SEQ - 1)]
        pltpu.make_async_copy(sent, sent, send_sem.at[c]).wait()
        sent = back.at[c, pl.ds(0, SEQ - 1)]
        pltpu.make_async_copy(sent, sent, back_send_sem.at[c]).wait()
        ag_copy(c).wait_send()
        rs_copy(c).wait_send()
    sp_copy.wait_send()
    for c in (CHUNKS - 2, CHUNKS - 1):
        for copy in out_copies(c):
            copy.wait()


def per_device(first_qkv, video_qkv, head_kind, out_weight):
    g = lax.axis_index("head")
    kinds = head_kind.reshape(4, LOCAL)
    orders = jnp.argsort(1 - kinds, axis=1, stable=True)
    order = lax.dynamic_index_in_dim(orders, g, 0, keepdims=False)
    first = first_qkv.reshape(3, 64, LOCAL, HEAD_DIM)
    kv = jnp.take(first[1:], order[:NS], axis=2).reshape(2, 64, SW)
    kv = lax.all_gather(kv, "seq", axis=1, tiled=True)
    rows = jnp.take(out_weight.reshape(LOCAL, HEAD_DIM, 96), order, axis=0).reshape(WIDTH, 96)
    rows = lax.all_gather(rows.T, "seq", axis=0, tiled=True)
    rows = lax.all_gather(rows, "head", axis=0).reshape(4, 4, WIDTH, WIDTH)

    def part(source, block):
        return lax.dynamic_slice(rows, (source, block, 0, 0), (1, 1, WIDTH, WIDTH))[0, 0]

    near = jnp.bitwise_xor(g, 1)
    weight = jnp.stack(
        [jnp.concatenate([part(g, b), part(near, b)], axis=1) for b in (g, 3 - g)]
    )
    bf16 = jnp.bfloat16
    any_spec = pl.BlockSpec(memory_space=pl.ANY)
    dma = pltpu.SemaphoreType.DMA
    first_out, video_out = pl.pallas_call(
        kernel,
        out_shape=(
            jax.ShapeDtypeStruct((64, WIDTH), bf16),
            jax.ShapeDtypeStruct((SEQ, 64, WIDTH), bf16),
        ),
        in_specs=[pl.BlockSpec(memory_space=pltpu.SMEM)] + [any_spec] * 4,
        out_specs=(any_spec, any_spec),
        scratch_shapes=[
            pltpu.VMEM((3, 64, WIDTH), bf16),
            pltpu.VMEM((2, 3, SEQ, TILE, WIDTH), bf16),
            pltpu.VMEM((3, NS, F, HEAD_DIM), bf16),
            pltpu.VMEM((2, F, SW), bf16),
            pltpu.VMEM((2, WIDTH, 2 * WIDTH), bf16),
            pltpu.VMEM((CHUNKS, SEQ, 3, TILE, TW), bf16),
            pltpu.VMEM((CHUNKS, FRAMES, 3, TILE, TW), bf16),
            pltpu.VMEM((CHUNKS, FRAMES, TILE, TW), bf16),
            pltpu.VMEM((CHUNKS, FRAMES, TILE, 2 * WIDTH), bf16),
            pltpu.VMEM((CHUNKS, FRAMES, TILE, WIDTH), bf16),
            pltpu.VMEM((CHUNKS, FRAMES, TILE, WIDTH), bf16),
            pltpu.VMEM((2, FRAMES, TILE, WIDTH), bf16),
            pltpu.VMEM((TILE, ROWS), jnp.float32),
            dma((2,)), dma((3,)), dma((CHUNKS,)), dma((CHUNKS,)), dma((CHUNKS,)), dma((CHUNKS,)),
            dma, dma, dma((CHUNKS,)), dma((CHUNKS,)), dma((CHUNKS,)), dma((CHUNKS,)), dma((2, 2)),
        ],
        compiler_params=pltpu.CompilerParams(
            collective_id=0, has_side_effects=True, vmem_limit_bytes=62 * 2**20
        ),
        name="denoise_attention",
    )(head_kind, first_qkv, video_qkv.reshape(3, SEQ, 64, WIDTH), kv, weight)
    return first_out, video_out.reshape(F, WIDTH)


def solution(mesh):
    in_specs = (P(None, "seq", "head"), P(None, "seq", "head"), P(), P("head", "seq"))
    out_specs = (P("seq", "head"), P("seq", "head"))
    return jax.shard_map(
        per_device, mesh=mesh, in_specs=in_specs, out_specs=out_specs, check_vma=False
    )
```

```python
import functools

import jax
import jax.numpy as jnp
from jax import lax
from jax.experimental import pallas as pl
from jax.experimental.pallas import tpu as pltpu
from jax.sharding import PartitionSpec as P

HEAD_DIM = 128
F = 2048
SEQ = 32
LOCAL = 6
NS = 2
NT = 4
CHUNKS = 4
TILE = 16
WIDTH = LOCAL * HEAD_DIM
SW = NS * HEAD_DIM
TW = NT * HEAD_DIM
FRAMES = SEQ + 1
SHARD = 96
ROWS = FRAMES * TILE
EXP_SCALE = HEAD_DIM ** (-0.5) * 1.4426950408889634
MASKED = -1e30
MESH = pl.DeviceIdType.MESH
NT_DIMS = (((1,), (1,)), ((), ()))


def kernel(
    kinds, first_hbm, video_hbm, w_hbm, first_out, video_out,
    first, stage, spatial, kv, shard_in, shard, weight, send, recv, back, act, part_send, part_recv, out_buf, bias,
    load_sem, const_sem, send_sem, recv_sem, back_send_sem, back_recv_sem,
    sp_send_sem, sp_recv_sem, ag_send_sem, ag_recv_sem, rs_send_sem, rs_recv_sem, out_sem,
    swap_sem, kv_send_sem, kv_recv_sem, w_send_sem, w_recv_sem,
):
    s = lax.axis_index("seq")
    g = lax.axis_index("head")
    near = jnp.bitwise_xor(g, 1)
    far = 3 - g
    y, z, core = s // 8, (s // 2) % 4, s % 2

    def load(c):
        return pltpu.make_async_copy(
            video_hbm.at[:, :, pl.ds(c * TILE, TILE)], stage.at[c % 2], load_sem.at[c % 2]
        )

    load(0).start()
    load(1).start()
    first_copy = pltpu.make_async_copy(first_hbm, first, const_sem.at[0])
    first_copy.start()
    shard_copy = pltpu.make_async_copy(w_hbm, shard_in, const_sem.at[1])
    shard_copy.start()

    barrier = pltpu.get_barrier_semaphore()

    def greet(k, carry):
        pl.semaphore_signal(
            barrier, inc=1, device_id=(jnp.bitwise_xor(s, k), g), device_id_type=MESH
        )
        return carry

    lax.fori_loop(1, SEQ, greet, 0)
    for other in (near, far):
        pl.semaphore_signal(barrier, inc=1, device_id=(s, other), device_id_type=MESH)

    kind = [kinds[g * LOCAL + h] for h in range(LOCAL)]
    takes = []
    for slot in range(LOCAL):
        want, rank = (1, slot) if slot < NS else (0, slot - NS)
        seen = jnp.int32(0)
        row = []
        for h in range(LOCAL):
            is_kind = kind[h] == want
            row.append(jnp.logical_and(is_kind, seen == rank))
            seen = seen + jnp.where(is_kind, 1, 0)
        takes.append(row)

    def pick(slot, heads):
        low, count = (slot, 5) if slot < NS else (slot - NS, 3)
        value = heads[low]
        for h in range(low + 1, low + count):
            value = lax.select(takes[slot][h], heads[h], value)
        return value

    def split(tile):
        return [tile[:, h * HEAD_DIM : (h + 1) * HEAD_DIM] for h in range(LOCAL)]

    row_id = lax.broadcasted_iota(jnp.int32, (TILE, ROWS), 0)
    col_id = lax.broadcasted_iota(jnp.int32, (TILE, ROWS), 1)
    bias[...] = jnp.where(row_id == jnp.bitwise_and(col_id, TILE - 1), 0.0, MASKED)

    first_copy.wait()
    for c in range(CHUNKS):
        for plane in range(3):
            heads = split(first[plane, c * TILE : (c + 1) * TILE, :])
            for slot in range(NT):
                recv[c, 0, plane, :, slot * HEAD_DIM : (slot + 1) * HEAD_DIM] = pick(
                    NS + slot, heads
                )
            if plane == 0:
                for slot in range(NS):
                    act[c, 0, :, slot * HEAD_DIM : (slot + 1) * HEAD_DIM] = pick(slot, heads)
            else:
                for slot in range(NS):
                    kv[
                        y, z, core, plane - 1, c * TILE : (c + 1) * TILE,
                        slot * HEAD_DIM : (slot + 1) * HEAD_DIM,
                    ] = pick(slot, heads)

    shard_copy.wait()
    for r in range(0, SHARD, TILE):
        heads = split(shard_in[r : r + TILE, :])
        for slot in range(LOCAL):
            shard[r : r + TILE, slot * HEAD_DIM : (slot + 1) * HEAD_DIM] = pick(slot, heads)

    def outer(n):
        return jnp.logical_or(n == 0, n == 3)

    stays = outer(y) == outer(g)
    own_block = jnp.where(y == g, 0, 1)
    near_block = jnp.where(y == near, 0, 1)
    low, high = pl.ds(0, WIDTH), pl.ds(WIDTH, WIDTH)

    def swap_copy(block):
        return pltpu.make_async_remote_copy(
            src_ref=shard, dst_ref=weight.at[block, z, core, :, high],
            send_sem=swap_sem.at[0], recv_sem=swap_sem.at[1],
            device_id=(s, near), device_id_type=MESH,
        )

    def to_seq(source, target, send_sem_, recv_sem_):
        pltpu.make_async_remote_copy(
            src_ref=source, dst_ref=source, send_sem=send_sem_, recv_sem=recv_sem_,
            device_id=(target, g), device_id_type=MESH,
        ).start()

    def along_z(source, send_sem_, recv_sem_):
        for k in range(1, 4):
            to_seq(source, y * 8 + ((z + k) % 4) * 2 + core, send_sem_, recv_sem_)

    def along_y(source, send_sem_, recv_sem_):
        for k in range(1, 4):
            to_seq(source, ((y + k) % 4) * 8 + z * 2 + core, send_sem_, recv_sem_)

    def across(source, send_sem_, recv_sem_):
        to_seq(source, s + 1 - 2 * core, send_sem_, recv_sem_)

    def await_bytes(ref, sem):
        pltpu.make_async_copy(ref, ref, sem).wait()

    def swap_start():
        @pl.when(jnp.logical_not(stays))
        def _():
            swap_copy(near_block).start()

        @pl.when(stays)
        def _():
            weight[own_block, z, core, :, 0:WIDTH] = shard[...]

    def kv_first():
        @pl.when(core == 0)
        def _():
            along_z(kv.at[y, z, core], kv_send_sem.at[0], kv_recv_sem.at[0])

        @pl.when(core == 1)
        def _():
            along_y(kv.at[y, z, core], kv_send_sem.at[0], kv_recv_sem.at[0])

    def kv_second():
        await_bytes(kv.at[y, pl.ds(0, 3), core], kv_recv_sem.at[0])

        @pl.when(core == 0)
        def _():
            along_y(kv.at[y, :, core], kv_send_sem.at[1], kv_recv_sem.at[1])

        @pl.when(core == 1)
        def _():
            along_z(kv.at[:, z, core], kv_send_sem.at[1], kv_recv_sem.at[1])

    def kv_third():
        await_bytes(kv.at[pl.ds(0, 3), :, core], kv_recv_sem.at[1])
        across(kv.at[:, :, core], kv_send_sem.at[2], kv_recv_sem.at[2])

    def w_first():
        @pl.when(stays)
        def _():
            swap_copy(own_block).wait_recv()

            @pl.when(core == 0)
            def _():
                along_z(weight.at[own_block, z, core], w_send_sem.at[0], w_recv_sem.at[0])

            @pl.when(core == 1)
            def _():
                along_y(weight.at[own_block, z, core], w_send_sem.at[0], w_recv_sem.at[0])

    def w_second():
        @pl.when(core == 0)
        def _():
            @pl.when(stays)
            def _():
                await_bytes(weight.at[own_block, pl.ds(0, 3), core], w_recv_sem.at[0])
                along_y(weight.at[own_block, :, core], w_send_sem.at[1], w_recv_sem.at[1])

        @pl.when(core == 1)
        def _():
            @pl.when(stays)
            def _():
                await_bytes(weight.at[0, z, core], w_recv_sem.at[0])

            @pl.when(jnp.logical_not(stays))
            def _():
                await_bytes(weight.at[:, z, core], w_recv_sem.at[0])

            along_z(weight.at[:, z, core], w_send_sem.at[1], w_recv_sem.at[1])

    def w_third():
        @pl.when(core == 0)
        def _():
            @pl.when(stays)
            def _():
                await_bytes(weight.at[0, :, core], w_recv_sem.at[1])

            @pl.when(jnp.logical_not(stays))
            def _():
                await_bytes(weight.at[:, :, core], w_recv_sem.at[1])

        @pl.when(core == 1)
        def _():
            await_bytes(weight.at[:, pl.ds(0, 3), core], w_recv_sem.at[1])

        across(weight.at[:, :, core], w_send_sem.at[2], w_recv_sem.at[2])

    def spread_sent():
        await_bytes(kv.at[0, pl.ds(0, 3), core], kv_send_sem.at[0])
        await_bytes(kv.at[pl.ds(0, 3), :, core], kv_send_sem.at[1])
        await_bytes(kv.at[:, :, core], kv_send_sem.at[2])
        await_bytes(weight.at[:, :, core], w_send_sem.at[2])

        @pl.when(jnp.logical_not(stays))
        def _():
            swap_copy(near_block).wait_send()

        @pl.when(stays)
        def _():
            await_bytes(weight.at[0, pl.ds(0, 3), core], w_send_sem.at[0])

        @pl.when(jnp.logical_and(stays, core == 0))
        def _():
            for _k in range(3):
                await_bytes(weight.at[0, :, core], w_send_sem.at[1])

        @pl.when(core == 1)
        def _():
            await_bytes(weight.at[:, pl.ds(0, 3), core], w_send_sem.at[1])

    pl.semaphore_wait(barrier, SEQ + 1)
    swap_start()
    kv_first()

    def pack_and_post(c):
        load(c).wait()

        def pack(d, carry):
            for plane in range(3):
                heads = split(stage[c % 2, plane, d])
                for slot in range(NT):
                    send[c, d, plane, :, slot * HEAD_DIM : (slot + 1) * HEAD_DIM] = pick(
                        NS + slot, heads
                    )
                start = pl.multiple_of(d * (CHUNKS * TILE) + c * TILE, TILE)
                for slot in range(NS):
                    spatial[plane, slot, pl.ds(start, TILE), :] = pick(slot, heads)
            return carry

        lax.fori_loop(0, SEQ, pack, 0)
        if c + 2 < CHUNKS:
            load(c + 2).start()

        def post(k, carry):
            d = jnp.bitwise_xor(s, k)
            pltpu.make_async_remote_copy(
                src_ref=send.at[c, d], dst_ref=recv.at[c, 1 + s],
                send_sem=send_sem.at[c], recv_sem=recv_sem.at[c],
                device_id=(d, g), device_id_type=MESH,
            ).start()
            return carry

        lax.fori_loop(1, SEQ, post, 0)
        pltpu.make_async_copy(send.at[c, s], recv.at[c, 1 + s], recv_sem.at[c]).start()

    pack_and_post(0)
    pack_and_post(1)
    w_first()
    kv_second()
    pack_and_post(2)
    pack_and_post(3)

    def attend(q, k, v, mask):
        scores = lax.dot_general(q, k, NT_DIMS, preferred_element_type=jnp.float32)
        if mask is not None:
            scores = (scores.reshape(FRAMES, TILE, ROWS) + mask[None]).reshape(ROWS, ROWS)
        top = jnp.max(scores, axis=-1, keepdims=True)
        raised = jnp.exp2((scores - top) * EXP_SCALE)
        total = jnp.sum(raised, axis=-1, keepdims=True)
        mixed = jnp.dot(raised.astype(jnp.bfloat16), v, preferred_element_type=jnp.float32)
        return (mixed / total).astype(jnp.bfloat16)

    block = 256
    for h in range(NS):
        columns = slice(h * HEAD_DIM, (h + 1) * HEAD_DIM)

        def frame_block(b, carry):
            start = pl.multiple_of(b * block, block)
            mixed = attend(spatial[0, h, pl.ds(start, block), :], spatial[1, h], spatial[2, h], None)
            for dd in range(block // (CHUNKS * TILE)):
                for c in range(CHUNKS):
                    at = (dd * CHUNKS + c) * TILE
                    act[c, 1 + b * (block // (CHUNKS * TILE)) + dd, :, columns] = mixed[at : at + TILE]
            return carry

        lax.fori_loop(0, F // block, frame_block, 0)
        if h == 0:
            w_second()
            kv_third()
        else:
            w_third()

    await_bytes(kv.at[:, :, core], kv_recv_sem.at[2])
    for h in range(NS):
        columns = slice(h * HEAD_DIM, (h + 1) * HEAD_DIM)
        queries = act[:, 0, :, columns].reshape(CHUNKS * TILE, HEAD_DIM)
        mixed = attend(
            queries,
            kv[:, :, :, 0, :, columns].reshape(F, HEAD_DIM),
            kv[:, :, :, 1, :, columns].reshape(F, HEAD_DIM),
            None,
        )
        for c in range(CHUNKS):
            act[c, 0, :, columns] = mixed[c * TILE : (c + 1) * TILE]

    sp_copy = pltpu.make_async_remote_copy(
        src_ref=act.at[:, :, :, pl.ds(0, SW)], dst_ref=act.at[:, :, :, pl.ds(WIDTH, SW)],
        send_sem=sp_send_sem, recv_sem=sp_recv_sem,
        device_id=(s, near), device_id_type=MESH,
    )
    sp_copy.start()

    def temporal(c):
        pltpu.make_async_copy(
            recv.at[c, pl.ds(1, SEQ)], recv.at[c, pl.ds(1, SEQ)], recv_sem.at[c]
        ).wait()

        def one_head(t, carry):
            columns = pl.ds(pl.multiple_of(t * HEAD_DIM, HEAD_DIM), HEAD_DIM)
            q, k, v = (
                recv[c, :, plane, :, columns].reshape(ROWS, HEAD_DIM) for plane in range(3)
            )
            mixed = attend(q, k, v, bias[...])
            back[c, :, :, columns] = mixed.reshape(FRAMES, TILE, HEAD_DIM)
            return carry

        lax.fori_loop(0, NT, one_head, 0)

        def post(k, carry):
            d = jnp.bitwise_xor(s, k)
            pltpu.make_async_remote_copy(
                src_ref=back.at[c, 1 + d], dst_ref=act.at[c, 1 + s, :, pl.ds(SW, TW)],
                send_sem=back_send_sem.at[c], recv_sem=back_recv_sem.at[c],
                device_id=(d, g), device_id_type=MESH,
            ).start()
            return carry

        lax.fori_loop(1, SEQ, post, 0)
        pltpu.make_async_copy(
            back.at[c, 1 + s], act.at[c, 1 + s, :, pl.ds(SW, TW)], back_recv_sem.at[c]
        ).start()
        act[c, 0, :, SW:WIDTH] = back[c, 0]

    def ag_copy(c):
        return pltpu.make_async_remote_copy(
            src_ref=act.at[c, :, :, pl.ds(SW, TW)], dst_ref=act.at[c, :, :, pl.ds(WIDTH + SW, TW)],
            send_sem=ag_send_sem.at[c], recv_sem=ag_recv_sem.at[c],
            device_id=(s, near), device_id_type=MESH,
        )

    def share(c):
        landed = act.at[c, pl.ds(1, SEQ), :, pl.ds(SW, TW)]
        pltpu.make_async_copy(landed, landed, back_recv_sem.at[c]).wait()
        ag_copy(c).start()

    def rs_copy(c):
        return pltpu.make_async_remote_copy(
            src_ref=part_send.at[c], dst_ref=part_recv.at[c],
            send_sem=rs_send_sem.at[c], recv_sem=rs_recv_sem.at[c],
            device_id=(s, far), device_id_type=MESH,
        )

    def project(c, which):
        return lax.dot_general(
            act[c].reshape(ROWS, 2 * WIDTH), weight[which].reshape(WIDTH, 2 * WIDTH), NT_DIMS,
            preferred_element_type=jnp.float32,
        )

    def partial(c):
        if c == 0:
            sp_copy.wait_recv()
            await_bytes(weight.at[:, :, core], w_recv_sem.at[2])
        ag_copy(c).wait_recv()
        part_send[c] = project(c, 1).astype(jnp.bfloat16).reshape(FRAMES, TILE, WIDTH)
        rs_copy(c).start()

    def out_copies(c):
        return (
            pltpu.make_async_copy(
                out_buf.at[c % 2, pl.ds(1, SEQ)], video_out.at[:, pl.ds(c * TILE, TILE)],
                out_sem.at[c % 2, 0],
            ),
            pltpu.make_async_copy(
                out_buf.at[c % 2, 0], first_out.at[pl.ds(c * TILE, TILE)], out_sem.at[c % 2, 1]
            ),
        )

    def finish(c):
        rs_copy(c).wait_recv()
        if c >= 2:
            for copy in out_copies(c - 2):
                copy.wait()
        total = project(c, 0) + part_recv[c].reshape(ROWS, WIDTH).astype(jnp.float32)
        out_buf[c % 2] = total.astype(jnp.bfloat16).reshape(FRAMES, TILE, WIDTH)
        for copy in out_copies(c):
            copy.start()

    for step in range(CHUNKS + 3):
        if step < CHUNKS:
            temporal(step)
        if 0 <= step - 1 < CHUNKS:
            share(step - 1)
        if 0 <= step - 2 < CHUNKS:
            partial(step - 2)
        if 0 <= step - 3 < CHUNKS:
            finish(step - 3)

    for c in range(CHUNKS):
        sent = send.at[c, pl.ds(0, SEQ - 1)]
        pltpu.make_async_copy(sent, sent, send_sem.at[c]).wait()
        sent = back.at[c, pl.ds(0, SEQ - 1)]
        pltpu.make_async_copy(sent, sent, back_send_sem.at[c]).wait()
        ag_copy(c).wait_send()
        rs_copy(c).wait_send()
    sp_copy.wait_send()
    spread_sent()
    for c in (CHUNKS - 2, CHUNKS - 1):
        for copy in out_copies(c):
            copy.wait()


def per_device(first_qkv, video_qkv, head_kind, out_weight):
    bf16 = jnp.bfloat16
    any_spec = pl.BlockSpec(memory_space=pl.ANY)
    dma = pltpu.SemaphoreType.DMA
    first_out, video_out = pl.pallas_call(
        kernel,
        out_shape=(
            jax.ShapeDtypeStruct((64, WIDTH), bf16),
            jax.ShapeDtypeStruct((SEQ, 64, WIDTH), bf16),
        ),
        in_specs=[pl.BlockSpec(memory_space=pltpu.SMEM)] + [any_spec] * 3,
        out_specs=(any_spec, any_spec),
        scratch_shapes=[
            pltpu.VMEM((3, 64, WIDTH), bf16),
            pltpu.VMEM((2, 3, SEQ, TILE, WIDTH), bf16),
            pltpu.VMEM((3, NS, F, HEAD_DIM), bf16),
            pltpu.VMEM((4, 4, 2, 2, 64, SW), bf16),
            pltpu.VMEM((SHARD, WIDTH), bf16),
            pltpu.VMEM((SHARD, WIDTH), bf16),
            pltpu.VMEM((2, 4, 2, SHARD, 2 * WIDTH), bf16),
            pltpu.VMEM((CHUNKS, SEQ, 3, TILE, TW), bf16),
            pltpu.VMEM((CHUNKS, FRAMES, 3, TILE, TW), bf16),
            pltpu.VMEM((CHUNKS, FRAMES, TILE, TW), bf16),
            pltpu.VMEM((CHUNKS, FRAMES, TILE, 2 * WIDTH), bf16),
            pltpu.VMEM((CHUNKS, FRAMES, TILE, WIDTH), bf16),
            pltpu.VMEM((CHUNKS, FRAMES, TILE, WIDTH), bf16),
            pltpu.VMEM((2, FRAMES, TILE, WIDTH), bf16),
            pltpu.VMEM((TILE, ROWS), jnp.float32),
            dma((2,)), dma((2,)), dma((CHUNKS,)), dma((CHUNKS,)), dma((CHUNKS,)), dma((CHUNKS,)),
            dma, dma, dma((CHUNKS,)), dma((CHUNKS,)), dma((CHUNKS,)), dma((CHUNKS,)), dma((2, 2)),
            dma((2,)), dma((3,)), dma((3,)), dma((3,)), dma((3,)),
        ],
        compiler_params=pltpu.CompilerParams(
            collective_id=0, has_side_effects=True, vmem_limit_bytes=62 * 2**20
        ),
        name="denoise_attention",
    )(head_kind, first_qkv, video_qkv.reshape(3, SEQ, 64, WIDTH), out_weight.T)
    return first_out, video_out.reshape(F, WIDTH)


def solution(mesh):
    in_specs = (P(None, "seq", "head"), P(None, "seq", "head"), P(), P("head", "seq"))
    out_specs = (P("seq", "head"), P("seq", "head"))
    return jax.shard_map(
        per_device, mesh=mesh, in_specs=in_specs, out_specs=out_specs, check_vma=False
    )
```

```python
import functools

import jax
import jax.numpy as jnp
from jax import lax
from jax.experimental import pallas as pl
from jax.experimental.pallas import tpu as pltpu
from jax.sharding import PartitionSpec as P

HEAD_DIM = 128
F = 2048
SEQ = 32
LOCAL = 6
NS = 2
NT = 4
PAIRS = 4
CHUNKS = 2 * PAIRS
TILE = 16
HALF = 8
WIDTH = LOCAL * HEAD_DIM
SW = NS * HEAD_DIM
TW = 2 * HEAD_DIM
FRAMES = SEQ + 1
SHARD = 96
ROWS = FRAMES * TILE
HALF_ROWS = FRAMES * HALF
EXP_SCALE = HEAD_DIM ** (-0.5) * 1.4426950408889634
MASKED = -1e30
MESH = pl.DeviceIdType.MESH
NT_DIMS = (((1,), (1,)), ((), ()))


def kernel(
    kinds, first_hbm, video_hbm, w_hbm, first_out, video_out,
    first, stage, spatial, kv, shard_in, shard, weight, send, recv, back, own_s, near_s, own_t, near_t,
    part_send, part_recv, acc, out_buf, bias,
    load_sem, const_sem, send_sem, recv_sem, back_send_sem, back_recv_sem,
    sp_send_sem, sp_recv_sem, ag_send_sem, ag_recv_sem, rs_send_sem, rs_recv_sem, out_sem,
    swap_sem, kv_send_sem, kv_recv_sem, w_send_sem, w_recv_sem,
):
    s = lax.axis_index("seq")
    g = lax.axis_index("head")
    near = jnp.bitwise_xor(g, 1)
    far = 3 - g
    y, z, core = s // 8, (s // 2) % 4, s % 2

    def load(c):
        return pltpu.make_async_copy(
            video_hbm.at[:, :, pl.ds(c * TILE, TILE)], stage.at[c % 2], load_sem.at[c % 2]
        )

    load(0).start()
    load(1).start()
    first_copy = pltpu.make_async_copy(first_hbm, first, const_sem.at[0])
    first_copy.start()
    shard_copy = pltpu.make_async_copy(w_hbm, shard_in, const_sem.at[1])
    shard_copy.start()

    barrier = pltpu.get_barrier_semaphore()

    def greet(k, carry):
        pl.semaphore_signal(
            barrier, inc=1, device_id=(jnp.bitwise_xor(s, k), g), device_id_type=MESH
        )
        return carry

    lax.fori_loop(1, SEQ, greet, 0)
    mirror = jnp.bitwise_xor(y, 1)
    mirror_seq = mirror * 8 + z * 2 + core
    for other in ((s, near), (s, far), (mirror_seq, near)):
        pl.semaphore_signal(barrier, inc=1, device_id=other, device_id_type=MESH)

    kind = [kinds[g * LOCAL + h] for h in range(LOCAL)]
    takes = []
    for slot in range(LOCAL):
        want, rank = (1, slot) if slot < NS else (0, slot - NS)
        seen = jnp.int32(0)
        row = []
        for h in range(LOCAL):
            is_kind = kind[h] == want
            row.append(jnp.logical_and(is_kind, seen == rank))
            seen = seen + jnp.where(is_kind, 1, 0)
        takes.append(row)

    def pick(slot, heads):
        low, count = (slot, 5) if slot < NS else (slot - NS, 3)
        value = heads[low]
        for h in range(low + 1, low + count):
            value = lax.select(takes[slot][h], heads[h], value)
        return value

    f32, bf16 = jnp.float32, jnp.bfloat16

    def pack_tiles(heads):
        tiles = [pick(NS + slot, heads).astype(f32) for slot in range(NT)]
        packed = []
        for half in range(2):
            rows = slice(half * HALF, (half + 1) * HALF)
            sides = [jnp.concatenate([tiles[i][rows], tiles[i + 2][rows]], axis=0) for i in range(2)]
            packed.append(jnp.concatenate(sides, axis=1).astype(bf16))
        return packed

    def split(tile):
        return [tile[:, h * HEAD_DIM : (h + 1) * HEAD_DIM] for h in range(LOCAL)]

    row_id = lax.broadcasted_iota(jnp.int32, (TILE, ROWS), 0)
    col_id = lax.broadcasted_iota(jnp.int32, (TILE, ROWS), 1)
    bias[...] = jnp.where(row_id == jnp.bitwise_and(col_id, TILE - 1), 0.0, MASKED)

    first_copy.wait()
    for c in range(PAIRS):
        for plane in range(3):
            heads = split(first[plane, c * TILE : (c + 1) * TILE, :])
            for half, tile in enumerate(pack_tiles(heads)):
                recv[2 * c + half, 0, plane] = tile
            if plane == 0:
                for slot in range(NS):
                    own_s[c, 0, :, slot * HEAD_DIM : (slot + 1) * HEAD_DIM] = pick(slot, heads)
            else:
                for slot in range(NS):
                    kv[
                        y, z, core, plane - 1, c * TILE : (c + 1) * TILE,
                        slot * HEAD_DIM : (slot + 1) * HEAD_DIM,
                    ] = pick(slot, heads)

    shard_copy.wait()
    for r in range(0, SHARD, TILE):
        heads = split(shard_in[r : r + TILE, :])
        for slot in range(LOCAL):
            shard[r : r + TILE, slot * HEAD_DIM : (slot + 1) * HEAD_DIM] = pick(slot, heads)

    def outer(n):
        return jnp.logical_or(n == 0, n == 3)

    stays = outer(y) == outer(g)
    swap_copy = pltpu.make_async_remote_copy(
        src_ref=shard, dst_ref=weight.at[mirror, z, core],
        send_sem=swap_sem.at[0], recv_sem=swap_sem.at[1],
        device_id=(mirror_seq, near), device_id_type=MESH,
    )

    def swap_start():
        @pl.when(jnp.logical_not(stays))
        def _():
            swap_copy.start()

        @pl.when(stays)
        def _():
            weight[y, z, core] = shard[...]

    def swap_wait():
        @pl.when(jnp.logical_not(stays))
        def _():
            swap_copy.wait()

    def to_seq(ref, target, sems):
        pltpu.make_async_remote_copy(
            src_ref=ref, dst_ref=ref, send_sem=sems[0], recv_sem=sems[1],
            device_id=(target, g), device_id_type=MESH,
        ).start()

    def along_z(ref, sems):
        for k in range(1, 4):
            to_seq(ref, y * 8 + ((z + k) % 4) * 2 + core, sems)

    def along_y(ref, sems):
        for k in range(1, 4):
            to_seq(ref, ((y + k) % 4) * 8 + z * 2 + core, sems)

    def await_bytes(ref, sem):
        pltpu.make_async_copy(ref, ref, sem).wait()

    class Spread:
        def __init__(self, buf, send_sems, recv_sems):
            self.buf = buf
            self.sems = [(send_sems.at[i], recv_sems.at[i]) for i in range(3)]

        def first(self):
            @pl.when(core == 0)
            def _():
                along_z(self.buf.at[y, z, core], self.sems[0])

            @pl.when(core == 1)
            def _():
                along_y(self.buf.at[y, z, core], self.sems[0])

        def second(self):
            await_bytes(self.buf.at[0, pl.ds(0, 3), core], self.sems[0][1])

            @pl.when(core == 0)
            def _():
                along_y(self.buf.at[y, :, core], self.sems[1])

            @pl.when(core == 1)
            def _():
                along_z(self.buf.at[:, z, core], self.sems[1])

        def third(self):
            await_bytes(self.buf.at[pl.ds(0, 3), :, core], self.sems[1][1])
            to_seq(self.buf.at[:, :, core], s + 1 - 2 * core, self.sems[2])

        def arrived(self):
            await_bytes(self.buf.at[:, :, core], self.sems[2][1])

        def sent(self):
            await_bytes(self.buf.at[0, pl.ds(0, 3), core], self.sems[0][0])
            await_bytes(self.buf.at[pl.ds(0, 3), :, core], self.sems[1][0])
            await_bytes(self.buf.at[:, :, core], self.sems[2][0])

    kv_spread = Spread(kv, kv_send_sem, kv_recv_sem)
    w_spread = Spread(weight, w_send_sem, w_recv_sem)


    def pack_chunk(c):
        load(c).wait()

        def pack(d, carry):
            for plane in range(3):
                heads = split(stage[c % 2, plane, d])
                for half, tile in enumerate(pack_tiles(heads)):
                    send[2 * c + half, d, plane] = tile
                start = pl.multiple_of(d * (PAIRS * TILE) + c * TILE, TILE)
                for slot in range(NS):
                    spatial[plane, slot, pl.ds(start, TILE), :] = pick(slot, heads)
            return carry

        lax.fori_loop(0, SEQ, pack, 0)
        if c + 2 < PAIRS:
            load(c + 2).start()

    def peer(i):
        bits = (i % 2) * 16 + ((i // 2) % 2) * 8 + ((i // 4) % 2) * 4 + ((i // 8) % 2) * 2 + i // 16
        return jnp.bitwise_xor(s, bits)

    def post_chunk(c):
        def post(i, carry):
            d = peer(i)
            pltpu.make_async_remote_copy(
                src_ref=send.at[c, d], dst_ref=recv.at[c, 1 + s],
                send_sem=send_sem.at[c], recv_sem=recv_sem.at[c],
                device_id=(d, g), device_id_type=MESH,
            ).start()
            return carry

        lax.fori_loop(1, SEQ, post, 0)
        pltpu.make_async_copy(send.at[c, s], recv.at[c, 1 + s], recv_sem.at[c]).start()

    def attend(q, k, v, mask):
        scores = lax.dot_general(q, k, NT_DIMS, preferred_element_type=jnp.float32)
        if mask is not None:
            scores = (scores.reshape(FRAMES, TILE, ROWS) + mask[None]).reshape(ROWS, ROWS)
        top = jnp.max(scores, axis=-1, keepdims=True)
        raised = jnp.exp2((scores - top) * EXP_SCALE)
        total = jnp.sum(raised, axis=-1, keepdims=True)
        mixed = jnp.dot(raised.astype(jnp.bfloat16), v, preferred_element_type=jnp.float32)
        return (mixed / total).astype(jnp.bfloat16)

    def sp_copy(h):
        return pltpu.make_async_remote_copy(
            src_ref=own_s.at[:, pl.ds(1, SEQ), :, pl.ds(h * HEAD_DIM, HEAD_DIM)],
            dst_ref=near_s.at[:, pl.ds(1, SEQ), :, pl.ds(h * HEAD_DIM, HEAD_DIM)],
            send_sem=sp_send_sem.at[h], recv_sem=sp_recv_sem.at[h],
            device_id=(s, near), device_id_type=MESH,
        )

    first_share = pltpu.make_async_remote_copy(
        src_ref=own_s.at[:, 0], dst_ref=near_s.at[:, 0],
        send_sem=sp_send_sem.at[NS], recv_sem=sp_recv_sem.at[NS],
        device_id=(s, near), device_id_type=MESH,
    )

    block = 256

    def frame_head(h):
        columns = slice(h * HEAD_DIM, (h + 1) * HEAD_DIM)
        owners = block // (PAIRS * TILE)

        def frame_block(b, carry):
            start = pl.multiple_of(b * block, block)
            mixed = attend(spatial[0, h, pl.ds(start, block), :], spatial[1, h], spatial[2, h], None)
            for dd in range(owners):
                for c in range(PAIRS):
                    at = (dd * PAIRS + c) * TILE
                    own_s[c, 1 + b * owners + dd, :, columns] = mixed[at : at + TILE]
            return carry

        lax.fori_loop(0, F // block, frame_block, 0)
        sp_copy(h).start()

    def first_frame():
        kv_spread.arrived()
        for h in range(NS):
            columns = slice(h * HEAD_DIM, (h + 1) * HEAD_DIM)
            queries = own_s[:, 0, :, columns].reshape(PAIRS * TILE, HEAD_DIM)
            mixed = attend(
                queries,
                kv[:, :, :, 0, :, columns].reshape(F, HEAD_DIM),
                kv[:, :, :, 1, :, columns].reshape(F, HEAD_DIM),
                None,
            )
            for c in range(PAIRS):
                own_s[c, 0, :, columns] = mixed[c * TILE : (c + 1) * TILE]
        first_share.start()

    def temporal(c):
        pltpu.make_async_copy(
            recv.at[c, pl.ds(1, SEQ)], recv.at[c, pl.ds(1, SEQ)], recv_sem.at[c]
        ).wait()

        def one_head(t, carry):
            columns = pl.ds(pl.multiple_of(t * HEAD_DIM, HEAD_DIM), HEAD_DIM)
            q, k, v = (
                recv[c, :, plane, :, columns].reshape(ROWS, HEAD_DIM) for plane in range(3)
            )
            mixed = attend(q, k, v, bias[...])
            back[c, :, :, columns] = mixed.reshape(FRAMES, TILE, HEAD_DIM)
            return carry

        lax.fori_loop(0, 2, one_head, 0)

        def post(i, carry):
            d = peer(i)
            pltpu.make_async_remote_copy(
                src_ref=back.at[c, 1 + d], dst_ref=own_t.at[c, 1 + s],
                send_sem=back_send_sem.at[c], recv_sem=back_recv_sem.at[c],
                device_id=(d, g), device_id_type=MESH,
            ).start()
            return carry

        lax.fori_loop(1, SEQ, post, 0)
        pltpu.make_async_copy(
            back.at[c, 1 + s], own_t.at[c, 1 + s], back_recv_sem.at[c]
        ).start()
        own_t[c, 0] = back[c, 0]

    def ag_copy(c):
        return pltpu.make_async_remote_copy(
            src_ref=own_t.at[c], dst_ref=near_t.at[c],
            send_sem=ag_send_sem.at[c], recv_sem=ag_recv_sem.at[c],
            device_id=(s, near), device_id_type=MESH,
        )

    def share(c):
        landed = own_t.at[c, pl.ds(1, SEQ)]
        pltpu.make_async_copy(landed, landed, back_recv_sem.at[c]).wait()
        ag_copy(c).start()

    def rs_copy(c):
        return pltpu.make_async_remote_copy(
            src_ref=part_send.at[c], dst_ref=part_recv.at[c],
            send_sem=rs_send_sem.at[c], recv_sem=rs_recv_sem.at[c],
            device_id=(s, far), device_id_type=MESH,
        )

    def times(own, near_half, block):
        return sum(
            lax.dot_general(
                part.reshape(-1, WIDTH).astype(bf16), weight[at].reshape(WIDTH, WIDTH), NT_DIMS,
                preferred_element_type=f32,
            )
            for part, at in ((own, block), (near_half, jnp.bitwise_xor(block, 1)))
        )

    def half_rows(c, spatial_ref, temporal_ref):
        rows = slice((c % 2) * HALF, (c % 2 + 1) * HALF)
        mixed = temporal_ref[c].astype(f32)
        return jnp.concatenate(
            [spatial_ref[c // 2].astype(f32)[:, rows], mixed[:, :HALF], mixed[:, HALF:]], axis=2
        )

    def pair_rows(c, spatial_ref, temporal_ref):
        halves = [temporal_ref[2 * c + half].astype(f32) for half in range(2)]
        sides = [
            jnp.concatenate([half[:, rows] for half in halves], axis=1).astype(bf16)
            for rows in (slice(0, HALF), slice(HALF, TILE))
        ]
        return jnp.concatenate([spatial_ref[c]] + sides, axis=2)

    def partial(c):
        if c == 0:
            for h in range(NS):
                sp_copy(h).wait_recv()
            first_share.wait_recv()
            w_spread.arrived()
        ag_copy(c).wait_recv()
        part = times(half_rows(c, own_s, own_t), half_rows(c, near_s, near_t), far)
        part = part.reshape(FRAMES, HALF, WIDTH)
        part_send[c] = jnp.concatenate(
            [part[:, :, : WIDTH // 2], part[:, :, WIDTH // 2 :]], axis=1
        ).astype(bf16)
        rs_copy(c).start()

    def own_block(c):
        acc[...] = times(pair_rows(c, own_s, own_t), pair_rows(c, near_s, near_t), g).reshape(
            FRAMES, TILE, WIDTH
        )

    def out_copies(c):
        return (
            pltpu.make_async_copy(
                out_buf.at[c % 2, pl.ds(1, SEQ)], video_out.at[:, pl.ds(c * TILE, TILE)],
                out_sem.at[c % 2, 0],
            ),
            pltpu.make_async_copy(
                out_buf.at[c % 2, 0], first_out.at[pl.ds(c * TILE, TILE)], out_sem.at[c % 2, 1]
            ),
        )

    def finish(c):
        if c >= 2:
            for copy in out_copies(c - 2):
                copy.wait()
        halves = []
        for half in range(2):
            rs_copy(2 * c + half).wait_recv()
            part = part_recv[2 * c + half].astype(f32)
            halves.append(jnp.concatenate([part[:, :HALF], part[:, HALF:]], axis=2))
        out_buf[c % 2] = (acc[...] + jnp.concatenate(halves, axis=1)).astype(bf16)
        for copy in out_copies(c):
            copy.start()

    pack_chunk(0)
    pl.semaphore_wait(barrier, SEQ + 2)
    swap_start()
    kv_spread.first()
    post_chunk(0)
    swap_wait()
    w_spread.first()
    kv_spread.second()
    post_chunk(1)
    pack_chunk(1)
    pack_chunk(2)
    pack_chunk(3)
    w_spread.second()
    frame_head(0)
    temporal(0)
    post_chunk(2)
    kv_spread.third()
    frame_head(1)
    temporal(1)
    post_chunk(3)
    first_frame()
    w_spread.third()
    for step in range(2, CHUNKS):
        share(step - 2)
        temporal(step)
        if step + 2 < CHUNKS:
            post_chunk(step + 2)
        if step == CHUNKS - 1:
            share(CHUNKS - 2)
        partial(step - 2)
        if step == CHUNKS - 1:
            share(CHUNKS - 1)
        if step % 2 == 1:
            own_block((step - 3) // 2)
        elif step >= 4:
            finish((step - 4) // 2)
    partial(CHUNKS - 2)
    finish(PAIRS - 2)
    partial(CHUNKS - 1)
    own_block(PAIRS - 1)
    finish(PAIRS - 1)

    for c in range(CHUNKS):
        sent = send.at[c, pl.ds(0, SEQ - 1)]
        pltpu.make_async_copy(sent, sent, send_sem.at[c]).wait()
        sent = back.at[c, pl.ds(0, SEQ - 1)]
        pltpu.make_async_copy(sent, sent, back_send_sem.at[c]).wait()
        ag_copy(c).wait_send()
        rs_copy(c).wait_send()
    for h in range(NS):
        sp_copy(h).wait_send()
    first_share.wait_send()
    kv_spread.sent()
    w_spread.sent()
    for c in (PAIRS - 2, PAIRS - 1):
        for copy in out_copies(c):
            copy.wait()


def per_device(first_qkv, video_qkv, head_kind, out_weight):
    bf16 = jnp.bfloat16
    any_spec = pl.BlockSpec(memory_space=pl.ANY)
    dma = pltpu.SemaphoreType.DMA
    first_out, video_out = pl.pallas_call(
        kernel,
        out_shape=(
            jax.ShapeDtypeStruct((64, WIDTH), bf16),
            jax.ShapeDtypeStruct((SEQ, 64, WIDTH), bf16),
        ),
        in_specs=[pl.BlockSpec(memory_space=pltpu.SMEM)] + [any_spec] * 3,
        out_specs=(any_spec, any_spec),
        scratch_shapes=[
            pltpu.VMEM((3, 64, WIDTH), bf16),
            pltpu.VMEM((2, 3, SEQ, TILE, WIDTH), bf16),
            pltpu.VMEM((3, NS, F, HEAD_DIM), bf16),
            pltpu.VMEM((4, 4, 2, 2, 64, SW), bf16),
            pltpu.VMEM((SHARD, WIDTH), bf16),
            pltpu.VMEM((SHARD, WIDTH), bf16),
            pltpu.VMEM((4, 4, 2, SHARD, WIDTH), bf16),
            pltpu.VMEM((CHUNKS, SEQ, 3, TILE, TW), bf16),
            pltpu.VMEM((CHUNKS, FRAMES, 3, TILE, TW), bf16),
            pltpu.VMEM((CHUNKS, FRAMES, TILE, TW), bf16),
            pltpu.VMEM((PAIRS, FRAMES, TILE, SW), bf16),
            pltpu.VMEM((PAIRS, FRAMES, TILE, SW), bf16),
            pltpu.VMEM((CHUNKS, FRAMES, TILE, TW), bf16),
            pltpu.VMEM((CHUNKS, FRAMES, TILE, TW), bf16),
            pltpu.VMEM((CHUNKS, FRAMES, TILE, WIDTH // 2), bf16),
            pltpu.VMEM((CHUNKS, FRAMES, TILE, WIDTH // 2), bf16),
            pltpu.VMEM((FRAMES, TILE, WIDTH), jnp.float32),
            pltpu.VMEM((2, FRAMES, TILE, WIDTH), bf16),
            pltpu.VMEM((TILE, ROWS), jnp.float32),
            dma((2,)), dma((2,)), dma((CHUNKS,)), dma((CHUNKS,)), dma((CHUNKS,)), dma((CHUNKS,)),
            dma((NS + 1,)), dma((NS + 1,)), dma((CHUNKS,)), dma((CHUNKS,)), dma((CHUNKS,)), dma((CHUNKS,)), dma((2, 2)),
            dma((2,)), dma((3,)), dma((3,)), dma((3,)), dma((3,)),
        ],
        compiler_params=pltpu.CompilerParams(
            collective_id=0, has_side_effects=True, vmem_limit_bytes=62 * 2**20
        ),
        name="denoise_attention",
    )(head_kind, first_qkv, video_qkv.reshape(3, SEQ, 64, WIDTH), out_weight.T)
    return first_out, video_out.reshape(F, WIDTH)


def solution(mesh):
    in_specs = (P(None, "seq", "head"), P(None, "seq", "head"), P(), P("head", "seq"))
    out_specs = (P("seq", "head"), P("seq", "head"))
    return jax.shard_map(
        per_device, mesh=mesh, in_specs=in_specs, out_specs=out_specs, check_vma=False
    )
```

```python
import functools

import jax
import jax.numpy as jnp
from jax import lax
from jax.experimental import pallas as pl
from jax.experimental.pallas import tpu as pltpu
from jax.sharding import PartitionSpec as P

HEAD_DIM = 128
F = 2048
SEQ = 32
LOCAL = 6
NS = 2
NT = 4
PAIRS = 4
CHUNKS = 2 * PAIRS
TILE = 16
HALF = 8
WIDTH = LOCAL * HEAD_DIM
SW = NS * HEAD_DIM
TW = 2 * HEAD_DIM
FRAMES = SEQ + 1
SHARD = 96
SPLIT = 17
ROWS = FRAMES * TILE
HALF_ROWS = FRAMES * HALF
EXP_SCALE = HEAD_DIM ** (-0.5) * 1.4426950408889634
MASKED = -1e30
MESH = pl.DeviceIdType.MESH
NT_DIMS = (((1,), (1,)), ((), ()))


def kernel(
    kinds, first_hbm, video_hbm, w_hbm, first_out, video_out,
    first, stage, spatial, kv, shard_in, shard, weight, send, recv, back, own_s, near_s, own_t, near_t,
    part_send, part_recv, acc, out_buf, bias,
    load_sem, const_sem, send_sem, recv_sem, back_send_sem, back_recv_sem,
    sp_send_sem, sp_recv_sem, ag_send_sem, ag_recv_sem, rs_send_sem, rs_recv_sem, out_sem,
    swap_sem, kv_send_sem, kv_recv_sem, w_send_sem, w_recv_sem,
):
    s = lax.axis_index("seq")
    g = lax.axis_index("head")
    near = jnp.bitwise_xor(g, 1)
    far = 3 - g
    y, z, core = s // 8, (s // 2) % 4, s % 2

    def load(c):
        return pltpu.make_async_copy(
            video_hbm.at[:, :, pl.ds(c * TILE, TILE)], stage.at[c % 2], load_sem.at[c % 2]
        )

    load(0).start()
    load(1).start()
    first_copy = pltpu.make_async_copy(first_hbm, first, const_sem.at[0])
    first_copy.start()
    shard_copy = pltpu.make_async_copy(w_hbm, shard_in, const_sem.at[1])
    shard_copy.start()

    barrier = pltpu.get_barrier_semaphore()

    def greet(k, carry):
        pl.semaphore_signal(
            barrier, inc=1, device_id=(jnp.bitwise_xor(s, k), g), device_id_type=MESH
        )
        return carry

    lax.fori_loop(1, SEQ, greet, 0)
    mirror = jnp.bitwise_xor(y, 1)
    mirror_seq = mirror * 8 + z * 2 + core
    for other in ((s, near), (s, far), (mirror_seq, near)):
        pl.semaphore_signal(barrier, inc=1, device_id=other, device_id_type=MESH)

    kind = [kinds[g * LOCAL + h] for h in range(LOCAL)]
    takes = []
    for slot in range(LOCAL):
        want, rank = (1, slot) if slot < NS else (0, slot - NS)
        seen = jnp.int32(0)
        row = []
        for h in range(LOCAL):
            is_kind = kind[h] == want
            row.append(jnp.logical_and(is_kind, seen == rank))
            seen = seen + jnp.where(is_kind, 1, 0)
        takes.append(row)

    def pick(slot, heads):
        low, count = (slot, 5) if slot < NS else (slot - NS, 3)
        value = heads[low]
        for h in range(low + 1, low + count):
            value = lax.select(takes[slot][h], heads[h], value)
        return value

    f32, bf16 = jnp.float32, jnp.bfloat16

    def pack_tiles(heads):
        tiles = [pick(NS + slot, heads).astype(f32) for slot in range(NT)]
        packed = []
        for half in range(2):
            rows = slice(half * HALF, (half + 1) * HALF)
            sides = [jnp.concatenate([tiles[i][rows], tiles[i + 2][rows]], axis=0) for i in range(2)]
            packed.append(jnp.concatenate(sides, axis=1).astype(bf16))
        return packed

    def split(tile):
        return [tile[:, h * HEAD_DIM : (h + 1) * HEAD_DIM] for h in range(LOCAL)]

    row_id = lax.broadcasted_iota(jnp.int32, (TILE, ROWS), 0)
    col_id = lax.broadcasted_iota(jnp.int32, (TILE, ROWS), 1)
    bias[...] = jnp.where(row_id == jnp.bitwise_and(col_id, TILE - 1), 0.0, MASKED)

    first_copy.wait()
    for c in range(PAIRS):
        for plane in range(3):
            heads = split(first[plane, c * TILE : (c + 1) * TILE, :])
            for half, tile in enumerate(pack_tiles(heads)):
                recv[2 * c + half, 0, plane] = tile
            if plane == 0:
                for slot in range(NS):
                    own_s[c, 0, :, slot * HEAD_DIM : (slot + 1) * HEAD_DIM] = pick(slot, heads)
            else:
                for slot in range(NS):
                    kv[
                        y, z, core, plane - 1, c * TILE : (c + 1) * TILE,
                        slot * HEAD_DIM : (slot + 1) * HEAD_DIM,
                    ] = pick(slot, heads)

    shard_copy.wait()
    for r in range(0, SHARD, TILE):
        heads = split(shard_in[r : r + TILE, :])
        for slot in range(LOCAL):
            shard[r : r + TILE, slot * HEAD_DIM : (slot + 1) * HEAD_DIM] = pick(slot, heads)

    def outer(n):
        return jnp.logical_or(n == 0, n == 3)

    stays = outer(y) == outer(g)
    swap_copy = pltpu.make_async_remote_copy(
        src_ref=shard, dst_ref=weight.at[mirror, z, core],
        send_sem=swap_sem.at[0], recv_sem=swap_sem.at[1],
        device_id=(mirror_seq, near), device_id_type=MESH,
    )

    def swap_start():
        @pl.when(jnp.logical_not(stays))
        def _():
            swap_copy.start()

        @pl.when(stays)
        def _():
            weight[y, z, core] = shard[...]

    def swap_wait():
        @pl.when(jnp.logical_not(stays))
        def _():
            swap_copy.wait()

    def to_seq(ref, target, sems):
        pltpu.make_async_remote_copy(
            src_ref=ref, dst_ref=ref, send_sem=sems[0], recv_sem=sems[1],
            device_id=(target, g), device_id_type=MESH,
        ).start()

    def along_z(ref, sems):
        for k in range(1, 4):
            to_seq(ref, y * 8 + ((z + k) % 4) * 2 + core, sems)

    def along_y(ref, sems):
        for k in range(1, 4):
            to_seq(ref, ((y + k) % 4) * 8 + z * 2 + core, sems)

    def await_bytes(ref, sem):
        pltpu.make_async_copy(ref, ref, sem).wait()

    class Spread:
        def __init__(self, buf, send_sems, recv_sems):
            self.buf = buf
            self.sems = [(send_sems.at[i], recv_sems.at[i]) for i in range(3)]

        def first(self):
            @pl.when(core == 0)
            def _():
                along_z(self.buf.at[y, z, core], self.sems[0])

            @pl.when(core == 1)
            def _():
                along_y(self.buf.at[y, z, core], self.sems[0])

        def second(self):
            await_bytes(self.buf.at[0, pl.ds(0, 3), core], self.sems[0][1])

            @pl.when(core == 0)
            def _():
                along_y(self.buf.at[y, :, core], self.sems[1])

            @pl.when(core == 1)
            def _():
                along_z(self.buf.at[:, z, core], self.sems[1])

        def third(self):
            await_bytes(self.buf.at[pl.ds(0, 3), :, core], self.sems[1][1])
            to_seq(self.buf.at[:, :, core], s + 1 - 2 * core, self.sems[2])

        def arrived(self):
            await_bytes(self.buf.at[:, :, core], self.sems[2][1])

        def sent(self):
            await_bytes(self.buf.at[0, pl.ds(0, 3), core], self.sems[0][0])
            await_bytes(self.buf.at[pl.ds(0, 3), :, core], self.sems[1][0])
            await_bytes(self.buf.at[:, :, core], self.sems[2][0])

    kv_spread = Spread(kv, kv_send_sem, kv_recv_sem)
    w_spread = Spread(weight, w_send_sem, w_recv_sem)


    def pack_chunk(c):
        load(c).wait()

        def pack(d, carry):
            for plane in range(3):
                heads = split(stage[c % 2, plane, d])
                for half, tile in enumerate(pack_tiles(heads)):
                    send[2 * c + half, d, plane] = tile
                start = pl.multiple_of(d * (PAIRS * TILE) + c * TILE, TILE)
                for slot in range(NS):
                    spatial[plane, slot, pl.ds(start, TILE), :] = pick(slot, heads)
            return carry

        lax.fori_loop(0, SEQ, pack, 0)
        if c + 2 < PAIRS:
            load(c + 2).start()

    def peer(i):
        bits = (i % 2) * 16 + ((i // 2) % 2) * 8 + ((i // 4) % 2) * 4 + ((i // 8) % 2) * 2 + i // 16
        return jnp.bitwise_xor(s, bits)

    def post_chunk(c):
        def post(i, carry):
            d = peer(i)
            pltpu.make_async_remote_copy(
                src_ref=send.at[c, d], dst_ref=recv.at[c, 1 + s],
                send_sem=send_sem.at[c], recv_sem=recv_sem.at[c],
                device_id=(d, g), device_id_type=MESH,
            ).start()
            return carry

        lax.fori_loop(1, SEQ, post, 0)
        pltpu.make_async_copy(send.at[c, s], recv.at[c, 1 + s], recv_sem.at[c]).start()

    def attend(q, k, v, mask):
        scores = lax.dot_general(q, k, NT_DIMS, preferred_element_type=jnp.float32)
        if mask is not None:
            scores = (scores.reshape(FRAMES, TILE, ROWS) + mask[None]).reshape(ROWS, ROWS)
        top = jnp.max(scores, axis=-1, keepdims=True)
        raised = jnp.exp2((scores - top) * EXP_SCALE)
        total = jnp.sum(raised, axis=-1, keepdims=True)
        mixed = jnp.dot(raised.astype(jnp.bfloat16), v, preferred_element_type=jnp.float32)
        return (mixed / total).astype(jnp.bfloat16)

    def sp_copy(h):
        return pltpu.make_async_remote_copy(
            src_ref=own_s.at[:, pl.ds(1, SEQ), :, pl.ds(h * HEAD_DIM, HEAD_DIM)],
            dst_ref=near_s.at[:, pl.ds(1, SEQ), :, pl.ds(h * HEAD_DIM, HEAD_DIM)],
            send_sem=sp_send_sem.at[h], recv_sem=sp_recv_sem.at[h],
            device_id=(s, near), device_id_type=MESH,
        )

    first_share = pltpu.make_async_remote_copy(
        src_ref=own_s.at[:, 0], dst_ref=near_s.at[:, 0],
        send_sem=sp_send_sem.at[NS], recv_sem=sp_recv_sem.at[NS],
        device_id=(s, near), device_id_type=MESH,
    )

    block = 256

    def frame_head(h):
        columns = slice(h * HEAD_DIM, (h + 1) * HEAD_DIM)
        owners = block // (PAIRS * TILE)

        def frame_block(b, carry):
            start = pl.multiple_of(b * block, block)
            mixed = attend(spatial[0, h, pl.ds(start, block), :], spatial[1, h], spatial[2, h], None)
            for dd in range(owners):
                for c in range(PAIRS):
                    at = (dd * PAIRS + c) * TILE
                    own_s[c, 1 + b * owners + dd, :, columns] = mixed[at : at + TILE]
            return carry

        lax.fori_loop(0, F // block, frame_block, 0)
        sp_copy(h).start()

    def first_frame():
        kv_spread.arrived()
        for h in range(NS):
            columns = slice(h * HEAD_DIM, (h + 1) * HEAD_DIM)
            queries = own_s[:, 0, :, columns].reshape(PAIRS * TILE, HEAD_DIM)
            mixed = attend(
                queries,
                kv[:, :, :, 0, :, columns].reshape(F, HEAD_DIM),
                kv[:, :, :, 1, :, columns].reshape(F, HEAD_DIM),
                None,
            )
            for c in range(PAIRS):
                own_s[c, 0, :, columns] = mixed[c * TILE : (c + 1) * TILE]
        first_share.start()

    def temporal(c):
        pltpu.make_async_copy(
            recv.at[c, pl.ds(1, SEQ)], recv.at[c, pl.ds(1, SEQ)], recv_sem.at[c]
        ).wait()

        def one_head(t, carry):
            columns = pl.ds(pl.multiple_of(t * HEAD_DIM, HEAD_DIM), HEAD_DIM)
            q, k, v = (
                recv[c, :, plane, :, columns].reshape(ROWS, HEAD_DIM) for plane in range(3)
            )
            mixed = attend(q, k, v, bias[...])
            back[c, :, :, columns] = mixed.reshape(FRAMES, TILE, HEAD_DIM)
            return carry

        lax.fori_loop(0, 2, one_head, 0)

        def post(i, carry):
            d = peer(i)
            pltpu.make_async_remote_copy(
                src_ref=back.at[c, 1 + d], dst_ref=own_t.at[c, 1 + s],
                send_sem=back_send_sem.at[c], recv_sem=back_recv_sem.at[c],
                device_id=(d, g), device_id_type=MESH,
            ).start()
            return carry

        lax.fori_loop(1, SEQ, post, 0)
        pltpu.make_async_copy(
            back.at[c, 1 + s], own_t.at[c, 1 + s], back_recv_sem.at[c]
        ).start()
        own_t[c, 0] = back[c, 0]

    def pieces(c):
        return ((0, FRAMES),) if c < CHUNKS - 2 else ((0, SPLIT), (SPLIT, FRAMES - SPLIT))

    def ag_copy(c, i):
        at = pl.ds(*pieces(c)[i])
        return pltpu.make_async_remote_copy(
            src_ref=own_t.at[c, at], dst_ref=near_t.at[c, at],
            send_sem=ag_send_sem.at[c, i], recv_sem=ag_recv_sem.at[c, i],
            device_id=(s, near), device_id_type=MESH,
        )

    def share(c):
        landed = own_t.at[c, pl.ds(1, SEQ)]
        pltpu.make_async_copy(landed, landed, back_recv_sem.at[c]).wait()
        for i in range(len(pieces(c))):
            ag_copy(c, i).start()

    def rs_copy(c, i):
        at = pl.ds(*pieces(c)[i])
        return pltpu.make_async_remote_copy(
            src_ref=part_send.at[c, at], dst_ref=part_recv.at[c, at],
            send_sem=rs_send_sem.at[c, i], recv_sem=rs_recv_sem.at[c, i],
            device_id=(s, far), device_id_type=MESH,
        )

    def times(own, near_half, block):
        return sum(
            lax.dot_general(
                part.reshape(-1, WIDTH).astype(bf16), weight[at].reshape(WIDTH, WIDTH), NT_DIMS,
                preferred_element_type=f32,
            )
            for part, at in ((own, block), (near_half, jnp.bitwise_xor(block, 1)))
        )

    def half_rows(c, at, spatial_ref, temporal_ref):
        rows = slice((c % 2) * HALF, (c % 2 + 1) * HALF)
        mixed = temporal_ref[c, at].astype(f32)
        return jnp.concatenate(
            [spatial_ref[c // 2, at].astype(f32)[:, rows], mixed[:, :HALF], mixed[:, HALF:]], axis=2
        )

    def pair_rows(c, spatial_ref, temporal_ref):
        halves = [temporal_ref[2 * c + half].astype(f32) for half in range(2)]
        sides = [
            jnp.concatenate([half[:, rows] for half in halves], axis=1).astype(bf16)
            for rows in (slice(0, HALF), slice(HALF, TILE))
        ]
        return jnp.concatenate([spatial_ref[c]] + sides, axis=2)

    def partial(c):
        if c == 0:
            for h in range(NS):
                sp_copy(h).wait_recv()
            first_share.wait_recv()
            w_spread.arrived()
        for i, (low, count) in enumerate(pieces(c)):
            ag_copy(c, i).wait_recv()
            at = slice(low, low + count)
            part = times(half_rows(c, at, own_s, own_t), half_rows(c, at, near_s, near_t), far)
            part = part.reshape(count, HALF, WIDTH)
            part_send[c, at] = jnp.concatenate(
                [part[:, :, : WIDTH // 2], part[:, :, WIDTH // 2 :]], axis=1
            ).astype(bf16)
            rs_copy(c, i).start()

    def own_block(c):
        acc[...] = times(pair_rows(c, own_s, own_t), pair_rows(c, near_s, near_t), g).reshape(
            FRAMES, TILE, WIDTH
        )

    def out_copies(c):
        return (
            pltpu.make_async_copy(
                out_buf.at[c % 2, pl.ds(1, SEQ)], video_out.at[:, pl.ds(c * TILE, TILE)],
                out_sem.at[c % 2, 0],
            ),
            pltpu.make_async_copy(
                out_buf.at[c % 2, 0], first_out.at[pl.ds(c * TILE, TILE)], out_sem.at[c % 2, 1]
            ),
        )

    def finish(c):
        if c >= 2:
            for copy in out_copies(c - 2):
                copy.wait()
        halves = []
        for half in range(2):
            for i in range(len(pieces(2 * c + half))):
                rs_copy(2 * c + half, i).wait_recv()
            part = part_recv[2 * c + half].astype(f32)
            halves.append(jnp.concatenate([part[:, :HALF], part[:, HALF:]], axis=2))
        out_buf[c % 2] = (acc[...] + jnp.concatenate(halves, axis=1)).astype(bf16)
        for copy in out_copies(c):
            copy.start()

    pack_chunk(0)
    pl.semaphore_wait(barrier, SEQ + 2)
    swap_start()
    kv_spread.first()
    post_chunk(0)
    swap_wait()
    w_spread.first()
    kv_spread.second()
    post_chunk(1)
    pack_chunk(1)
    pack_chunk(2)
    pack_chunk(3)
    w_spread.second()
    frame_head(0)
    temporal(0)
    post_chunk(2)
    kv_spread.third()
    frame_head(1)
    temporal(1)
    post_chunk(3)
    first_frame()
    w_spread.third()
    for step in range(2, CHUNKS - 2):
        share(step - 2)
        temporal(step)
        if step + 2 < CHUNKS - 1:
            post_chunk(step + 2)
        partial(step - 2)
        if step % 2 == 1:
            own_block((step - 3) // 2)
        elif step >= 4:
            finish((step - 4) // 2)
    share(CHUNKS - 4)
    temporal(CHUNKS - 2)
    post_chunk(CHUNKS - 1)
    share(CHUNKS - 3)
    partial(CHUNKS - 4)
    finish(PAIRS - 3)
    share(CHUNKS - 2)
    partial(CHUNKS - 3)
    own_block(PAIRS - 2)
    temporal(CHUNKS - 1)
    partial(CHUNKS - 2)
    share(CHUNKS - 1)
    finish(PAIRS - 2)
    partial(CHUNKS - 1)
    own_block(PAIRS - 1)
    finish(PAIRS - 1)

    for c in range(CHUNKS):
        sent = send.at[c, pl.ds(0, SEQ - 1)]
        pltpu.make_async_copy(sent, sent, send_sem.at[c]).wait()
        sent = back.at[c, pl.ds(0, SEQ - 1)]
        pltpu.make_async_copy(sent, sent, back_send_sem.at[c]).wait()
        for i in range(len(pieces(c))):
            ag_copy(c, i).wait_send()
            rs_copy(c, i).wait_send()
    for h in range(NS):
        sp_copy(h).wait_send()
    first_share.wait_send()
    kv_spread.sent()
    w_spread.sent()
    for c in (PAIRS - 2, PAIRS - 1):
        for copy in out_copies(c):
            copy.wait()


def hand_over(first, video, first_out, video_out):
    first_out[...] = first[...]
    video_out[...] = video[...]


def per_device(first_qkv, video_qkv, head_kind, out_weight):
    bf16 = jnp.bfloat16
    any_spec = pl.BlockSpec(memory_space=pl.ANY)
    dma = pltpu.SemaphoreType.DMA
    first_out, video_out = pl.pallas_call(
        kernel,
        out_shape=(
            jax.ShapeDtypeStruct((64, WIDTH), bf16),
            jax.ShapeDtypeStruct((SEQ, 64, WIDTH), bf16),
        ),
        in_specs=[pl.BlockSpec(memory_space=pltpu.SMEM)] + [any_spec] * 3,
        out_specs=(any_spec, any_spec),
        scratch_shapes=[
            pltpu.VMEM((3, 64, WIDTH), bf16),
            pltpu.VMEM((2, 3, SEQ, TILE, WIDTH), bf16),
            pltpu.VMEM((3, NS, F, HEAD_DIM), bf16),
            pltpu.VMEM((4, 4, 2, 2, 64, SW), bf16),
            pltpu.VMEM((SHARD, WIDTH), bf16),
            pltpu.VMEM((SHARD, WIDTH), bf16),
            pltpu.VMEM((4, 4, 2, SHARD, WIDTH), bf16),
            pltpu.VMEM((CHUNKS, SEQ, 3, TILE, TW), bf16),
            pltpu.VMEM((CHUNKS, FRAMES, 3, TILE, TW), bf16),
            pltpu.VMEM((CHUNKS, FRAMES, TILE, TW), bf16),
            pltpu.VMEM((PAIRS, FRAMES, TILE, SW), bf16),
            pltpu.VMEM((PAIRS, FRAMES, TILE, SW), bf16),
            pltpu.VMEM((CHUNKS, FRAMES, TILE, TW), bf16),
            pltpu.VMEM((CHUNKS, FRAMES, TILE, TW), bf16),
            pltpu.VMEM((CHUNKS, FRAMES, TILE, WIDTH // 2), bf16),
            pltpu.VMEM((CHUNKS, FRAMES, TILE, WIDTH // 2), bf16),
            pltpu.VMEM((FRAMES, TILE, WIDTH), jnp.float32),
            pltpu.VMEM((2, FRAMES, TILE, WIDTH), bf16),
            pltpu.VMEM((TILE, ROWS), jnp.float32),
            dma((2,)), dma((2,)), dma((CHUNKS,)), dma((CHUNKS,)), dma((CHUNKS,)), dma((CHUNKS,)),
            dma((NS + 1,)), dma((NS + 1,)), dma((CHUNKS, 2)), dma((CHUNKS, 2)), dma((CHUNKS, 2)), dma((CHUNKS, 2)), dma((2, 2)),
            dma((2,)), dma((3,)), dma((3,)), dma((3,)), dma((3,)),
        ],
        compiler_params=pltpu.CompilerParams(
            collective_id=0, has_side_effects=True, vmem_limit_bytes=62 * 2**20
        ),
        name="denoise_attention",
    )(head_kind, first_qkv, video_qkv.reshape(3, SEQ, 64, WIDTH), out_weight.T)
    first_out, video_out = pl.pallas_call(
        hand_over,
        out_shape=(
            jax.ShapeDtypeStruct((64, WIDTH), bf16),
            jax.ShapeDtypeStruct((SEQ, 64, WIDTH), bf16),
        ),
        grid=(4,),
        in_specs=[
            pl.BlockSpec((16, WIDTH), lambda i: (i, 0)),
            pl.BlockSpec((SEQ // 4, 64, WIDTH), lambda i: (i, 0, 0)),
        ],
        out_specs=(
            pl.BlockSpec((16, WIDTH), lambda i: (i, 0)),
            pl.BlockSpec((SEQ // 4, 64, WIDTH), lambda i: (i, 0, 0)),
        ),
        name="hand_over",
    )(first_out, video_out)
    return first_out, video_out.reshape(F, WIDTH)


def solution(mesh):
    in_specs = (P(None, "seq", "head"), P(None, "seq", "head"), P(), P("head", "seq"))
    out_specs = (P("seq", "head"), P("seq", "head"))
    return jax.shard_map(
        per_device, mesh=mesh, in_specs=in_specs, out_specs=out_specs, check_vma=False
    )
```

```python
import functools

import jax
import jax.numpy as jnp
from jax import lax
from jax.experimental import pallas as pl
from jax.experimental.pallas import tpu as pltpu
from jax.sharding import PartitionSpec as P

HEAD_DIM = 128
F = 2048
SEQ = 32
LOCAL = 6
NS = 2
NT = 4
PAIRS = 4
CHUNKS = 2 * PAIRS
TILE = 16
HALF = 8
WIDTH = LOCAL * HEAD_DIM
SW = NS * HEAD_DIM
TW = 2 * HEAD_DIM
FRAMES = SEQ + 1
SHARD = 96
SPLIT = 17
ROWS = FRAMES * TILE
HALF_ROWS = FRAMES * HALF
EXP_SCALE = HEAD_DIM ** (-0.5) * 1.4426950408889634
MASKED = -1e30
MESH = pl.DeviceIdType.MESH
NT_DIMS = (((1,), (1,)), ((), ()))


def kernel(
    kinds, first_hbm, video_hbm, w_hbm, first_out, video_out,
    first, stage, spatial, kv, shard_in, shard, weight, send, recv, back, own_s, near_s, own_t, near_t,
    part_send, part_recv, acc, out_buf, bias,
    load_sem, const_sem, send_sem, recv_sem, back_send_sem, back_recv_sem,
    sp_send_sem, sp_recv_sem, ag_send_sem, ag_recv_sem, rs_send_sem, rs_recv_sem, out_sem,
    swap_sem, kv_send_sem, kv_recv_sem, w_send_sem, w_recv_sem,
):
    s = lax.axis_index("seq")
    g = lax.axis_index("head")
    near = jnp.bitwise_xor(g, 1)
    far = 3 - g
    y, z, core = s // 8, (s // 2) % 4, s % 2

    def load(c):
        return pltpu.make_async_copy(
            video_hbm.at[:, :, pl.ds(c * TILE, TILE)], stage.at[c % 2], load_sem.at[c % 2]
        )

    load(0).start()
    load(1).start()
    first_copy = pltpu.make_async_copy(first_hbm, first, const_sem.at[0])
    first_copy.start()
    shard_copy = pltpu.make_async_copy(w_hbm, shard_in, const_sem.at[1])
    shard_copy.start()

    barrier = pltpu.get_barrier_semaphore()

    def greet(k, carry):
        pl.semaphore_signal(
            barrier, inc=1, device_id=(jnp.bitwise_xor(s, k), g), device_id_type=MESH
        )
        return carry

    lax.fori_loop(1, SEQ, greet, 0)
    mirror = jnp.bitwise_xor(y, 1)
    mirror_seq = mirror * 8 + z * 2 + core
    for other in ((s, near), (s, far), (mirror_seq, near)):
        pl.semaphore_signal(barrier, inc=1, device_id=other, device_id_type=MESH)

    kind = [kinds[g * LOCAL + h] for h in range(LOCAL)]
    takes = []
    for slot in range(LOCAL):
        want, rank = (1, slot) if slot < NS else (0, slot - NS)
        seen = jnp.int32(0)
        row = []
        for h in range(LOCAL):
            is_kind = kind[h] == want
            row.append(jnp.logical_and(is_kind, seen == rank))
            seen = seen + jnp.where(is_kind, 1, 0)
        takes.append(row)

    def pick(slot, heads):
        low, count = (slot, 5) if slot < NS else (slot - NS, 3)
        value = heads[low]
        for h in range(low + 1, low + count):
            value = lax.select(takes[slot][h], heads[h], value)
        return value

    f32, bf16 = jnp.float32, jnp.bfloat16

    def pack_tiles(heads):
        tiles = [pick(NS + slot, heads).astype(f32) for slot in range(NT)]
        packed = []
        for half in range(2):
            rows = slice(half * HALF, (half + 1) * HALF)
            sides = [jnp.concatenate([tiles[i][rows], tiles[i + 2][rows]], axis=0) for i in range(2)]
            packed.append(jnp.concatenate(sides, axis=1).astype(bf16))
        return packed

    def split(tile):
        return [tile[:, h * HEAD_DIM : (h + 1) * HEAD_DIM] for h in range(LOCAL)]

    row_id = lax.broadcasted_iota(jnp.int32, (TILE, ROWS), 0)
    col_id = lax.broadcasted_iota(jnp.int32, (TILE, ROWS), 1)
    bias[...] = jnp.where(row_id == jnp.bitwise_and(col_id, TILE - 1), 0.0, MASKED)

    first_copy.wait()
    for c in range(PAIRS):
        for plane in range(3):
            heads = split(first[plane, c * TILE : (c + 1) * TILE, :])
            for half, tile in enumerate(pack_tiles(heads)):
                recv[2 * c + half, 0, plane] = tile
            if plane == 0:
                for slot in range(NS):
                    own_s[c, 0, :, slot * HEAD_DIM : (slot + 1) * HEAD_DIM] = pick(slot, heads)
            else:
                for slot in range(NS):
                    kv[
                        y, z, core, plane - 1, c * TILE : (c + 1) * TILE,
                        slot * HEAD_DIM : (slot + 1) * HEAD_DIM,
                    ] = pick(slot, heads)

    shard_copy.wait()
    for r in range(0, SHARD, TILE):
        heads = split(shard_in[r : r + TILE, :])
        for slot in range(LOCAL):
            shard[r : r + TILE, slot * HEAD_DIM : (slot + 1) * HEAD_DIM] = pick(slot, heads)

    def outer(n):
        return jnp.logical_or(n == 0, n == 3)

    stays = outer(y) == outer(g)
    swap_copy = pltpu.make_async_remote_copy(
        src_ref=shard, dst_ref=weight.at[mirror, z, core],
        send_sem=swap_sem.at[0], recv_sem=swap_sem.at[1],
        device_id=(mirror_seq, near), device_id_type=MESH,
    )

    def swap_start():
        @pl.when(jnp.logical_not(stays))
        def _():
            swap_copy.start()

        @pl.when(stays)
        def _():
            weight[y, z, core] = shard[...]

    def swap_wait():
        @pl.when(jnp.logical_not(stays))
        def _():
            swap_copy.wait()

    def to_seq(ref, target, sems):
        pltpu.make_async_remote_copy(
            src_ref=ref, dst_ref=ref, send_sem=sems[0], recv_sem=sems[1],
            device_id=(target, g), device_id_type=MESH,
        ).start()

    def on_z(k):
        return y * 8 + ((z + k) % 4) * 2 + core

    def on_y(k):
        return ((y + k) % 4) * 8 + z * 2 + core

    def along_z(ref, sems):
        for k in range(1, 4):
            to_seq(ref, on_z(k), sems)

    def along_y(ref, sems):
        for k in range(1, 4):
            to_seq(ref, on_y(k), sems)

    def await_bytes(ref, sem):
        pltpu.make_async_copy(ref, ref, sem).wait()

    class Spread:
        def __init__(self, buf, halves, send_sems, recv_sems):
            self.buf = buf
            self.halves = halves
            self.sems = [(send_sems.at[i], recv_sems.at[i]) for i in range(4)]

        def first(self):
            @pl.when(core == 0)
            def _():
                along_z(self.buf.at[y, z, core], self.sems[0])

            @pl.when(core == 1)
            def _():
                along_y(self.buf.at[y, z, core], self.sems[0])

        def second(self):
            await_bytes(self.buf.at[0, pl.ds(0, 3), core], self.sems[0][1])

            @pl.when(core == 0)
            def _():
                for k in (1, 3):
                    to_seq(self.buf.at[y, :, core], on_y(k), self.sems[1])

            @pl.when(core == 1)
            def _():
                for k in (1, 3):
                    to_seq(self.buf.at[:, z, core], on_z(k), self.sems[1])

        def relay(self):
            await_bytes(self.buf.at[pl.ds(0, 2), :, core], self.sems[1][1])

            @pl.when(core == 0)
            def _():
                for k, half in ((1, self.halves[0]), (3, self.halves[1])):
                    to_seq(self.buf.at[(y + 4 - k) % 4, :, core, *half], on_y(k), self.sems[3])

            @pl.when(core == 1)
            def _():
                for k, half in ((1, self.halves[0]), (3, self.halves[1])):
                    to_seq(self.buf.at[:, (z + 4 - k) % 4, core, *half], on_z(k), self.sems[3])

        def third(self):
            await_bytes(self.buf.at[0, :, core], self.sems[3][1])
            to_seq(self.buf.at[:, :, core], s + 1 - 2 * core, self.sems[2])

        def arrived(self):
            await_bytes(self.buf.at[:, :, core], self.sems[2][1])

        def sent(self):
            await_bytes(self.buf.at[0, pl.ds(0, 3), core], self.sems[0][0])
            await_bytes(self.buf.at[pl.ds(0, 2), :, core], self.sems[1][0])
            await_bytes(self.buf.at[0, :, core], self.sems[3][0])
            await_bytes(self.buf.at[:, :, core], self.sems[2][0])

    kv_spread = Spread(
        kv, [(slice(None), pl.ds(i * 32, 32)) for i in range(2)], kv_send_sem, kv_recv_sem
    )
    w_spread = Spread(
        weight, [(pl.ds(i * 48, 48),) for i in range(2)], w_send_sem, w_recv_sem
    )


    def pack_chunk(c):
        load(c).wait()

        def pack(d, carry):
            for plane in range(3):
                heads = split(stage[c % 2, plane, d])
                for half, tile in enumerate(pack_tiles(heads)):
                    send[2 * c + half, d, plane] = tile
                start = pl.multiple_of(d * (PAIRS * TILE) + c * TILE, TILE)
                for slot in range(NS):
                    spatial[plane, slot, pl.ds(start, TILE), :] = pick(slot, heads)
            return carry

        lax.fori_loop(0, SEQ, pack, 0)
        if c + 2 < PAIRS:
            load(c + 2).start()

    def peer(i):
        bits = (i % 2) * 16 + ((i // 2) % 2) * 8 + ((i // 4) % 2) * 4 + ((i // 8) % 2) * 2 + i // 16
        return jnp.bitwise_xor(s, bits)

    def post_chunk(c):
        def post(i, carry):
            d = peer(i)
            pltpu.make_async_remote_copy(
                src_ref=send.at[c, d], dst_ref=recv.at[c, 1 + s],
                send_sem=send_sem.at[c], recv_sem=recv_sem.at[c],
                device_id=(d, g), device_id_type=MESH,
            ).start()
            return carry

        lax.fori_loop(1, SEQ, post, 0)
        pltpu.make_async_copy(send.at[c, s], recv.at[c, 1 + s], recv_sem.at[c]).start()

    def attend(q, k, v, mask):
        scores = lax.dot_general(q, k, NT_DIMS, preferred_element_type=jnp.float32)
        if mask is not None:
            scores = (scores.reshape(FRAMES, TILE, ROWS) + mask[None]).reshape(ROWS, ROWS)
        top = jnp.max(scores, axis=-1, keepdims=True)
        raised = jnp.exp2((scores - top) * EXP_SCALE)
        total = jnp.sum(raised, axis=-1, keepdims=True)
        mixed = jnp.dot(raised.astype(jnp.bfloat16), v, preferred_element_type=jnp.float32)
        return (mixed / total).astype(jnp.bfloat16)

    def sp_copy(h):
        return pltpu.make_async_remote_copy(
            src_ref=own_s.at[:, pl.ds(1, SEQ), :, pl.ds(h * HEAD_DIM, HEAD_DIM)],
            dst_ref=near_s.at[:, pl.ds(1, SEQ), :, pl.ds(h * HEAD_DIM, HEAD_DIM)],
            send_sem=sp_send_sem.at[h], recv_sem=sp_recv_sem.at[h],
            device_id=(s, near), device_id_type=MESH,
        )

    first_share = pltpu.make_async_remote_copy(
        src_ref=own_s.at[:, 0], dst_ref=near_s.at[:, 0],
        send_sem=sp_send_sem.at[NS], recv_sem=sp_recv_sem.at[NS],
        device_id=(s, near), device_id_type=MESH,
    )

    block = 256

    def frame_head(h):
        columns = slice(h * HEAD_DIM, (h + 1) * HEAD_DIM)
        owners = block // (PAIRS * TILE)

        def frame_block(b, carry):
            start = pl.multiple_of(b * block, block)
            mixed = attend(spatial[0, h, pl.ds(start, block), :], spatial[1, h], spatial[2, h], None)
            for dd in range(owners):
                for c in range(PAIRS):
                    at = (dd * PAIRS + c) * TILE
                    own_s[c, 1 + b * owners + dd, :, columns] = mixed[at : at + TILE]
            return carry

        lax.fori_loop(0, F // block, frame_block, 0)
        sp_copy(h).start()

    def first_frame():
        kv_spread.arrived()
        for h in range(NS):
            columns = slice(h * HEAD_DIM, (h + 1) * HEAD_DIM)
            queries = own_s[:, 0, :, columns].reshape(PAIRS * TILE, HEAD_DIM)
            mixed = attend(
                queries,
                kv[:, :, :, 0, :, columns].reshape(F, HEAD_DIM),
                kv[:, :, :, 1, :, columns].reshape(F, HEAD_DIM),
                None,
            )
            for c in range(PAIRS):
                own_s[c, 0, :, columns] = mixed[c * TILE : (c + 1) * TILE]
        first_share.start()

    def temporal(c):
        pltpu.make_async_copy(
            recv.at[c, pl.ds(1, SEQ)], recv.at[c, pl.ds(1, SEQ)], recv_sem.at[c]
        ).wait()

        def one_head(t, carry):
            columns = pl.ds(pl.multiple_of(t * HEAD_DIM, HEAD_DIM), HEAD_DIM)
            q, k, v = (
                recv[c, :, plane, :, columns].reshape(ROWS, HEAD_DIM) for plane in range(3)
            )
            mixed = attend(q, k, v, bias[...])
            back[c, :, :, columns] = mixed.reshape(FRAMES, TILE, HEAD_DIM)
            return carry

        lax.fori_loop(0, 2, one_head, 0)

        def post(i, carry):
            d = peer(i)
            pltpu.make_async_remote_copy(
                src_ref=back.at[c, 1 + d], dst_ref=own_t.at[c, 1 + s],
                send_sem=back_send_sem.at[c], recv_sem=back_recv_sem.at[c],
                device_id=(d, g), device_id_type=MESH,
            ).start()
            return carry

        lax.fori_loop(1, SEQ, post, 0)
        pltpu.make_async_copy(
            back.at[c, 1 + s], own_t.at[c, 1 + s], back_recv_sem.at[c]
        ).start()
        own_t[c, 0] = back[c, 0]

    def pieces(c):
        return ((0, FRAMES),) if c < CHUNKS - 2 else ((0, SPLIT), (SPLIT, FRAMES - SPLIT))

    def ag_copy(c, i):
        at = pl.ds(*pieces(c)[i])
        return pltpu.make_async_remote_copy(
            src_ref=own_t.at[c, at], dst_ref=near_t.at[c, at],
            send_sem=ag_send_sem.at[c, i], recv_sem=ag_recv_sem.at[c, i],
            device_id=(s, near), device_id_type=MESH,
        )

    def share(c):
        landed = own_t.at[c, pl.ds(1, SEQ)]
        pltpu.make_async_copy(landed, landed, back_recv_sem.at[c]).wait()
        for i in range(len(pieces(c))):
            ag_copy(c, i).start()

    def rs_copy(c, i):
        at = pl.ds(*pieces(c)[i])
        return pltpu.make_async_remote_copy(
            src_ref=part_send.at[c, at], dst_ref=part_recv.at[c, at],
            send_sem=rs_send_sem.at[c, i], recv_sem=rs_recv_sem.at[c, i],
            device_id=(s, far), device_id_type=MESH,
        )

    def times(own, near_half, block):
        return sum(
            lax.dot_general(
                part.reshape(-1, WIDTH).astype(bf16), weight[at].reshape(WIDTH, WIDTH), NT_DIMS,
                preferred_element_type=f32,
            )
            for part, at in ((own, block), (near_half, jnp.bitwise_xor(block, 1)))
        )

    def half_rows(c, at, spatial_ref, temporal_ref):
        rows = slice((c % 2) * HALF, (c % 2 + 1) * HALF)
        mixed = temporal_ref[c, at].astype(f32)
        return jnp.concatenate(
            [spatial_ref[c // 2, at].astype(f32)[:, rows], mixed[:, :HALF], mixed[:, HALF:]], axis=2
        )

    def pair_rows(c, spatial_ref, temporal_ref):
        halves = [temporal_ref[2 * c + half].astype(f32) for half in range(2)]
        sides = [
            jnp.concatenate([half[:, rows] for half in halves], axis=1).astype(bf16)
            for rows in (slice(0, HALF), slice(HALF, TILE))
        ]
        return jnp.concatenate([spatial_ref[c]] + sides, axis=2)

    def partial(c):
        if c == 0:
            for h in range(NS):
                sp_copy(h).wait_recv()
            first_share.wait_recv()
            w_spread.arrived()
        for i, (low, count) in enumerate(pieces(c)):
            ag_copy(c, i).wait_recv()
            at = slice(low, low + count)
            part = times(half_rows(c, at, own_s, own_t), half_rows(c, at, near_s, near_t), far)
            part = part.reshape(count, HALF, WIDTH)
            part_send[c, at] = jnp.concatenate(
                [part[:, :, : WIDTH // 2], part[:, :, WIDTH // 2 :]], axis=1
            ).astype(bf16)
            rs_copy(c, i).start()

    def own_block(c):
        acc[...] = times(pair_rows(c, own_s, own_t), pair_rows(c, near_s, near_t), g).reshape(
            FRAMES, TILE, WIDTH
        )

    def out_copies(c):
        return (
            pltpu.make_async_copy(
                out_buf.at[c % 2, pl.ds(1, SEQ)], video_out.at[:, pl.ds(c * TILE, TILE)],
                out_sem.at[c % 2, 0],
            ),
            pltpu.make_async_copy(
                out_buf.at[c % 2, 0], first_out.at[pl.ds(c * TILE, TILE)], out_sem.at[c % 2, 1]
            ),
        )

    def finish(c):
        if c >= 2:
            for copy in out_copies(c - 2):
                copy.wait()
        halves = []
        for half in range(2):
            for i in range(len(pieces(2 * c + half))):
                rs_copy(2 * c + half, i).wait_recv()
            part = part_recv[2 * c + half].astype(f32)
            halves.append(jnp.concatenate([part[:, :HALF], part[:, HALF:]], axis=2))
        out_buf[c % 2] = (acc[...] + jnp.concatenate(halves, axis=1)).astype(bf16)
        for copy in out_copies(c):
            copy.start()

    pack_chunk(0)
    pl.semaphore_wait(barrier, SEQ + 2)
    swap_start()
    kv_spread.first()
    post_chunk(0)
    swap_wait()
    w_spread.first()
    kv_spread.second()
    post_chunk(1)
    pack_chunk(1)
    pack_chunk(2)
    pack_chunk(3)
    w_spread.second()
    frame_head(0)
    kv_spread.relay()
    temporal(0)
    post_chunk(2)
    frame_head(1)
    w_spread.relay()
    kv_spread.third()
    temporal(1)
    post_chunk(3)
    first_frame()
    w_spread.third()
    for step in range(2, CHUNKS - 2):
        share(step - 2)
        temporal(step)
        if step + 2 < CHUNKS - 1:
            post_chunk(step + 2)
        partial(step - 2)
        if step % 2 == 1:
            own_block((step - 3) // 2)
        elif step >= 4:
            finish((step - 4) // 2)
    share(CHUNKS - 4)
    temporal(CHUNKS - 2)
    post_chunk(CHUNKS - 1)
    share(CHUNKS - 3)
    partial(CHUNKS - 4)
    finish(PAIRS - 3)
    share(CHUNKS - 2)
    partial(CHUNKS - 3)
    own_block(PAIRS - 2)
    temporal(CHUNKS - 1)
    partial(CHUNKS - 2)
    share(CHUNKS - 1)
    finish(PAIRS - 2)
    partial(CHUNKS - 1)
    own_block(PAIRS - 1)
    finish(PAIRS - 1)

    for c in range(CHUNKS):
        sent = send.at[c, pl.ds(0, SEQ - 1)]
        pltpu.make_async_copy(sent, sent, send_sem.at[c]).wait()
        sent = back.at[c, pl.ds(0, SEQ - 1)]
        pltpu.make_async_copy(sent, sent, back_send_sem.at[c]).wait()
        for i in range(len(pieces(c))):
            ag_copy(c, i).wait_send()
            rs_copy(c, i).wait_send()
    for h in range(NS):
        sp_copy(h).wait_send()
    first_share.wait_send()
    kv_spread.sent()
    w_spread.sent()
    for c in (PAIRS - 2, PAIRS - 1):
        for copy in out_copies(c):
            copy.wait()


def hand_over(first, video, first_out, video_out):
    first_out[...] = first[...]
    video_out[...] = video[...]


def per_device(first_qkv, video_qkv, head_kind, out_weight):
    bf16 = jnp.bfloat16
    any_spec = pl.BlockSpec(memory_space=pl.ANY)
    dma = pltpu.SemaphoreType.DMA
    first_out, video_out = pl.pallas_call(
        kernel,
        out_shape=(
            jax.ShapeDtypeStruct((64, WIDTH), bf16),
            jax.ShapeDtypeStruct((SEQ, 64, WIDTH), bf16),
        ),
        in_specs=[pl.BlockSpec(memory_space=pltpu.SMEM)] + [any_spec] * 3,
        out_specs=(any_spec, any_spec),
        scratch_shapes=[
            pltpu.VMEM((3, 64, WIDTH), bf16),
            pltpu.VMEM((2, 3, SEQ, TILE, WIDTH), bf16),
            pltpu.VMEM((3, NS, F, HEAD_DIM), bf16),
            pltpu.VMEM((4, 4, 2, 2, 64, SW), bf16),
            pltpu.VMEM((SHARD, WIDTH), bf16),
            pltpu.VMEM((SHARD, WIDTH), bf16),
            pltpu.VMEM((4, 4, 2, SHARD, WIDTH), bf16),
            pltpu.VMEM((CHUNKS, SEQ, 3, TILE, TW), bf16),
            pltpu.VMEM((CHUNKS, FRAMES, 3, TILE, TW), bf16),
            pltpu.VMEM((CHUNKS, FRAMES, TILE, TW), bf16),
            pltpu.VMEM((PAIRS, FRAMES, TILE, SW), bf16),
            pltpu.VMEM((PAIRS, FRAMES, TILE, SW), bf16),
            pltpu.VMEM((CHUNKS, FRAMES, TILE, TW), bf16),
            pltpu.VMEM((CHUNKS, FRAMES, TILE, TW), bf16),
            pltpu.VMEM((CHUNKS, FRAMES, TILE, WIDTH // 2), bf16),
            pltpu.VMEM((CHUNKS, FRAMES, TILE, WIDTH // 2), bf16),
            pltpu.VMEM((FRAMES, TILE, WIDTH), jnp.float32),
            pltpu.VMEM((2, FRAMES, TILE, WIDTH), bf16),
            pltpu.VMEM((TILE, ROWS), jnp.float32),
            dma((2,)), dma((2,)), dma((CHUNKS,)), dma((CHUNKS,)), dma((CHUNKS,)), dma((CHUNKS,)),
            dma((NS + 1,)), dma((NS + 1,)), dma((CHUNKS, 2)), dma((CHUNKS, 2)), dma((CHUNKS, 2)), dma((CHUNKS, 2)), dma((2, 2)),
            dma((2,)), dma((4,)), dma((4,)), dma((4,)), dma((4,)),
        ],
        compiler_params=pltpu.CompilerParams(
            collective_id=0, has_side_effects=True, vmem_limit_bytes=62 * 2**20
        ),
        name="denoise_attention",
    )(head_kind, first_qkv, video_qkv.reshape(3, SEQ, 64, WIDTH), out_weight.T)
    first_out, video_out = pl.pallas_call(
        hand_over,
        out_shape=(
            jax.ShapeDtypeStruct((64, WIDTH), bf16),
            jax.ShapeDtypeStruct((SEQ, 64, WIDTH), bf16),
        ),
        grid=(4,),
        in_specs=[
            pl.BlockSpec((16, WIDTH), lambda i: (i, 0)),
            pl.BlockSpec((SEQ // 4, 64, WIDTH), lambda i: (i, 0, 0)),
        ],
        out_specs=(
            pl.BlockSpec((16, WIDTH), lambda i: (i, 0)),
            pl.BlockSpec((SEQ // 4, 64, WIDTH), lambda i: (i, 0, 0)),
        ),
        name="hand_over",
    )(first_out, video_out)
    return first_out, video_out.reshape(F, WIDTH)


def solution(mesh):
    in_specs = (P(None, "seq", "head"), P(None, "seq", "head"), P(), P("head", "seq"))
    out_specs = (P("seq", "head"), P("seq", "head"))
    return jax.shard_map(
        per_device, mesh=mesh, in_specs=in_specs, out_specs=out_specs, check_vma=False
    )
```
